256 devices in a mesh: grid: 16 (over z, x_lo), sta: 16 (over y, x_hi, core).
Axes of the slice: x: 4 (x_hi: 2, x_lo: 2; x = x_hi * 2 + x_lo), y: 4, z: 8, core: 2. Of those that a mesh axis runs over, the one named last changes fastest.
Arguments:
- u_now: float32 [2048, 4096], P('grid', 'sta'), may hold values from -6 to 6
- u_prev: float32 [2048, 4096], P('grid', 'sta'), may hold values from -6 to 6
- buoyancy: float32 [2048, 4096], P('grid', 'sta'), may hold values from 0.5 to 1
- modulus: float32 [2048, 4096], P('grid', 'sta'), may hold values from 0.2 to 0.45
- station_cell: int32 [32768], P(('grid', 'sta')), may hold values from 0 to 8388607, as said below
- path_class: int32 [32768, 2048], P(('grid', 'sta')), may hold values from 0 to 7
- spectra: bfloat16 [2048, 512], P('sta'), may hold values from 0.099609375 to 1
- cos_table: float32 [2048, 512], P('sta')
- sin_table: float32 [2048, 512], P('sta')
- path_filter: float32 [8, 512], replicated, may hold values from 0.1 to 2
- lf_basis: float32 [4, 1024], replicated, may hold values from -3 to 3
- crossover: float32 [512], replicated, may hold values from 0.05 to 0.95
Outputs:
- broadband: float32 [32768, 1024], P(('grid', 'sta'))
- u_final: float32 [2048, 4096], P('grid', 'sta')
The draws below stay inside these ranges and needn't reach their ends.
Inputs may be any that keep to these rules, and one draw needn't show every extreme that they name: `station_cell`: station i lies in the columns of grid block ((i // 128) % 16) along the second dimension; its cell is row * 4096 + column.
All inputs are finite; a program needn't handle non-finite values.
Results may differ from the reference program's by a relative error of at most 0.0033.
Values may be sent and summed in bfloat16 or wider, within the bound.
A program may use at most 64 MiB of HBM per device.

```python
import math
import jax
import jax.numpy as jnp
from jax import lax

CY = 256
STA_DEV = 128
SUB_DEV = 128
STEPS = 4
NF = 512
CLASSES = 8
NX = 2048
NY = 4096
STATIONS = 32768
SUBFAULTS = 2048
N_STA = 16


def phase_angles(key):
    return jax.random.uniform(key, (SUBFAULTS, NF), jnp.float32, -math.pi, math.pi)


def draw_cos_table(key, part):
    return jnp.cos(phase_angles(key))


def draw_sin_table(key, part):
    return jnp.sin(phase_angles(key))


def draw_station_cell(key, part):
    key = jax.random.fold_in(key, 7)
    key_row, key_col = jax.random.split(key)
    index = jnp.arange(STATIONS, dtype=jnp.int32)
    column = index // STA_DEV % N_STA
    rows = jax.random.randint(key_row, (STATIONS,), 0, NX, dtype=jnp.int32)
    inside = jax.random.randint(key_col, (STATIONS,), 0, CY, dtype=jnp.int32)
    return (rows * NY + column * CY + inside).astype(jnp.int32)


def with_ends(drawn, rng, smallest, top_value):
    place = [jax.random.randint(jax.random.fold_in(rng, axis), (), 0, length) for axis, length in enumerate(drawn.shape)]
    widest = drawn.shape.index(max(drawn.shape))
    next_to = place[:widest] + [(place[widest] + 1) % drawn.shape[widest]] + place[widest + 1:]
    return drawn.at[tuple(place)].set(smallest).at[tuple(next_to)].set(top_value)


def level_of(own_key, extent, cuts, least, high):
    level, own = 1.0, jax.random.fold_in(own_key, 6)
    for axis_at, parts in cuts:
        draws = jnp.exp(jax.random.uniform(jax.random.fold_in(own, axis_at), (parts,), jnp.float32, least / len(cuts), high / len(cuts)))
        level = level * jnp.repeat(draws, extent[axis_at] // parts).reshape([-1 if axis == axis_at else 1 for axis in range(len(extent))])
    return level


def bell_draw(stream_key, extent, width, most, cuts=(), kind=jnp.bfloat16):
    values = jax.random.normal(stream_key, extent, jnp.float32) * width
    if len(cuts) > 0:
        values = level_of(stream_key, extent, cuts, -0.22, 0.18) * values
    return jnp.clip(values, min=-most, max=most).astype(kind)


def setup_inputs(seed: int = 0) -> dict:
    keys = jax.random.split(jax.random.key(seed), 13)
    u_now = bell_draw(keys[0], (NX, NY), 1.0, 6.0, ((0, 16), (1, 16)), jnp.float32)
    u_prev = bell_draw(keys[1], (NX, NY), 1.0, 6.0, ((0, 16), (1, 16)), jnp.float32)
    buoyancy = jnp.clip(jnp.exp(math.log(1.0) - 0.6931472 * jax.random.uniform(keys[2], (NX, NY), jnp.float32) ** level_of(keys[2], (NX, NY), ((0, 16), (1, 16)), -0.2, 0.2)), 0.5, 1.0)
    modulus = jnp.clip(jnp.exp(math.log(0.45) - 0.8109302 * jax.random.uniform(keys[3], (NX, NY), jnp.float32) ** level_of(keys[3], (NX, NY), ((0, 16), (1, 16)), -0.2, 0.2)), 0.2, 0.45)
    station_cell = draw_station_cell(jax.random.fold_in(keys[12], 71), 0)
    path_class = with_ends(jax.random.randint(keys[5], (STATIONS, SUBFAULTS), 0, CLASSES), jax.random.fold_in(keys[5], 1), 0, CLASSES - 1).astype(jnp.int32)
    spectra = jnp.clip(jnp.exp(math.log(1.0) - 2.306499 * jax.random.uniform(keys[6], (SUBFAULTS, NF), jnp.float32) ** level_of(keys[6], (SUBFAULTS, NF), ((0, 16),), -0.2, 0.2)), 0.099609375, 1.0).astype(jnp.bfloat16)
    cos_table = draw_cos_table(jax.random.fold_in(keys[12], 71), 0)
    sin_table = draw_sin_table(jax.random.fold_in(keys[12], 71), 0)
    path_filter = jnp.clip(jnp.exp(jax.random.uniform(keys[9], (CLASSES, NF), jnp.float32, math.log(0.1), math.log(2.0))), 0.1, 2.0)
    lf_basis = bell_draw(keys[10], (STEPS, 2 * NF), STEPS ** -0.5, 3.0, (), jnp.float32)
    crossover = jnp.clip(jax.random.uniform(keys[11], (NF,), jnp.float32, 0.05, 0.95), 0.05, 0.95)
    return dict(u_now=u_now, u_prev=u_prev, buoyancy=buoyancy, modulus=modulus, station_cell=station_cell, path_class=path_class, spectra=spectra, cos_table=cos_table, sin_table=sin_table, path_filter=path_filter, lf_basis=lf_basis, crossover=crossover)


def divergence(padu, padm):
    center = padu[1:-1, 1:-1]
    mid = padm[1:-1, 1:-1]
    right = 0.5 * (mid + padm[2:, 1:-1]) * (padu[2:, 1:-1] - center)
    left = 0.5 * (mid + padm[:-2, 1:-1]) * (center - padu[:-2, 1:-1])
    upper = 0.5 * (mid + padm[1:-1, 2:]) * (padu[1:-1, 2:] - center)
    lower = 0.5 * (mid + padm[1:-1, :-2]) * (center - padu[1:-1, :-2])
    return right - left + upper - lower

def contribution(classes, piece, doubled):
    count = piece.shape[0]
    levels = jnp.arange(CLASSES, dtype=jnp.int32)
    onehot = (classes[:, :, None] == levels[None, None, :]).astype(jnp.bfloat16)
    onehot = onehot.reshape(classes.shape[0], count * CLASSES)
    terms = (piece.astype(jnp.float32)[:, None, :] * doubled[None, :, :]).astype(jnp.bfloat16)
    terms = terms.reshape(count * CLASSES, doubled.shape[1])
    return jnp.dot(onehot, terms, preferred_element_type=jnp.float32)

def merging(low, high, crossover):
    lowpass = jnp.concatenate([crossover, crossover])[None, :]
    weight = lowpass * (1.0 - lowpass)
    numer = lax.optimization_barrier(jnp.mean(weight * low * low, axis=1))
    denom = lax.optimization_barrier(jnp.mean(weight * high * high, axis=1))
    ratio = jnp.sqrt((numer + 1e-06) / (denom + 1e-06))
    return lowpass * low + (1.0 - lowpass) * ratio[:, None] * high

def reference(u_now, u_prev, buoyancy, modulus, station_cell, path_class, spectra, cos_table, sin_table, path_filter, lf_basis, crossover):
    padm = jnp.pad(modulus, 1)
    current, previous = (u_now, u_prev)
    recorded = []
    for step in range(STEPS):
        following = 2.0 * current - previous + buoyancy * divergence(jnp.pad(current, 1), padm)
        previous, current = (current, following)
        recorded.append(current.reshape(-1)[station_cell])
    samples = jnp.stack(recorded)
    low = jnp.dot(samples.T, lf_basis, precision=lax.Precision.HIGHEST, preferred_element_type=jnp.float32)
    wide = spectra.astype(jnp.float32)
    phased = jnp.concatenate([wide * cos_table, wide * sin_table], axis=1).astype(jnp.bfloat16)
    doubled = jnp.concatenate([path_filter, path_filter], axis=1)

    def add_block(index, total):
        start = (index * SUB_DEV).astype(jnp.int32)
        piece = lax.dynamic_slice_in_dim(phased, start, SUB_DEV, 0)
        classes = lax.dynamic_slice_in_dim(path_class, start, SUB_DEV, 1)
        return total + contribution(classes, piece, doubled)
    high = lax.fori_loop(0, SUBFAULTS // SUB_DEV, add_block, jnp.zeros((STATIONS, 2 * NF), jnp.float32))
    return (merging(low, high, crossover), current)
```

```python
import functools

import jax
import jax.numpy as jnp
from jax import lax
from jax.experimental import pallas as pl
from jax.experimental.pallas import tpu as pltpu
from jax.sharding import PartitionSpec as P

STEPS = 4
CLASSES = 8
MESH = pl.DeviceIdType.MESH
BF16 = jnp.bfloat16
F32 = jnp.float32

SLOTS = ((0, 0), (0, 1), (1, 0), (3, 0), (1, 1), (3, 1), (2, 0), (2, 1))
FAR = [(dy, cross, dc) for dy, cross in SLOTS[1:] for dc in (0, 1)]
HALO = [(-1, 0), (1, 0), (0, -1), (0, 1), (-1, -1), (-1, 1), (1, -1), (1, 1)]
GRID = 16
SUBCHIP = 256


def kernel(
    u_ref,
    up_ref,
    b_ref,
    m_ref,
    cell_ref,
    class_ref,
    spectra_ref,
    cos_ref,
    sin_ref,
    filter_ref,
    basis_ref,
    cross_ref,
    out_ref,
    ufinal_ref,
    cells,
    cellsrc,
    rowsrc,
    colsrc,
    rowin,
    colin,
    cornerin,
    ext,
    ush,
    sampsrc,
    sampin,
    classown,
    classsib,
    onehot,
    phased,
    pieces,
    high,
    highin,
    cell_send,
    cell_recv,
    halo_send,
    halo_recv,
    samp_send,
    samp_recv,
    far_send,
    far_recv,
    sib_send,
    sib_recv,
):
    g = lax.axis_index("grid")
    s = lax.axis_index("sta")
    z, xl = g // 2, g % 2
    y, xh, core = s // 4, (s // 2) % 2, s % 2

    def along_grid(r):
        return ((g + r) % GRID, s)

    def beside(dg, ds):
        return ((g + dg + 16) % 16, (s + ds + 16) % 16)

    def chip(dy, cross, dc):
        xh2 = (xh + cross) % 2
        xl2 = (xl + cross) % 2
        return (z * 2 + xl2, (((y + dy) % 4) * 2 + xh2) * 2 + (core + dc) % 2)

    sibling = chip(0, 0, 1)
    partners = [along_grid(r) for r in range(1, GRID)]
    partners += [beside(*o) for o in HALO]
    partners += [chip(*o) for o in FAR]
    partners += [sibling]
    barrier = pltpu.get_barrier_semaphore()
    for partner in partners:
        pl.semaphore_signal(barrier, inc=1, device_id=partner, device_id_type=MESH)

    cellsrc[...] = jnp.broadcast_to(cell_ref[...], (8, 128))
    lane = lax.broadcasted_iota(jnp.int32, (128, 128), 1)
    packed = jnp.zeros((128, 128), F32)
    for a, ref in enumerate((u_ref, up_ref, b_ref, m_ref)):
        rowsrc[0, a] = ref[0:8, :]
        rowsrc[1, a] = ref[120:128, :]
        both = jnp.where(lane < 64, ref[:, 0:128], ref[:, 128:256])
        packed = jnp.where(lane // 8 == a, pltpu.roll(both, 8 * a + 4, 1), packed)
    colsrc[...] = jnp.transpose(packed)[0:32].reshape(4, 8, 128)
    wide = spectra_ref[...].astype(F32)
    phased[0] = (wide * cos_ref[...]).astype(BF16)
    phased[1] = (wide * sin_ref[...]).astype(BF16)
    for slot, (dy, cross) in enumerate(SLOTS):
        source = ((y + dy) % 4) * 2 + (xh + cross) % 2
        columns = pl.ds(pl.multiple_of(source * SUBCHIP, SUBCHIP), SUBCHIP)
        classown[:, slot * SUBCHIP : (slot + 1) * SUBCHIP] = (
            class_ref[:, columns].astype(F32).astype(BF16)
        )

    pl.semaphore_wait(barrier, len(partners))

    def remote(src, dst, send, recv, target):
        return pltpu.make_async_remote_copy(
            src_ref=src, dst_ref=dst, send_sem=send, recv_sem=recv, device_id=target, device_id_type=MESH
        )

    halo_copies = []
    for i, (dg, ds) in enumerate(HALO):
        if ds == 0:
            side = 1 if dg == 1 else 0
            src, dst = rowsrc.at[side], rowin.at[side]
        elif dg == 0:
            src, dst = colsrc, colin.at[1 if ds == 1 else 0]
        else:
            side = 1 if dg == 1 else 0
            half = 1 if ds == 1 else 0
            src = rowsrc.at[side, :, :, pl.ds(half * 128, 128)]
            dst = cornerin.at[side * 2 + half]
        halo_copies.append(remote(src, dst, halo_send.at[i], halo_recv.at[i], beside(dg, ds)))
    cell_copies = [
        remote(cellsrc, cells.at[GRID - r], cell_send.at[r], cell_recv.at[r], along_grid(r)) for r in range(1, GRID)
    ]
    far_copies = []
    for i, (dy, cross, dc) in enumerate(FAR):
        slot = SLOTS.index(((4 - dy) % 4, cross))
        far_copies.append(
            remote(
                phased.at[(core + dc) % 2],
                pieces.at[slot, pl.ds(pl.multiple_of(core * 128, 128), 128)],
                far_send.at[i],
                far_recv.at[i],
                chip(dy, cross, dc),
            )
        )
    sib_piece = remote(
        phased.at[1 - core],
        pieces.at[0, pl.ds(pl.multiple_of(core * 128, 128), 128)],
        sib_send.at[0],
        sib_recv.at[0],
        sibling,
    )
    sib_class = remote(classown, classsib, sib_send.at[1], sib_recv.at[1], sibling)
    for copy in halo_copies + cell_copies + [sib_class, sib_piece] + far_copies:
        copy.start()

    pieces[0, pl.ds(pl.multiple_of(core * 128, 128), 128)] = phased[core]
    cells[0] = cellsrc[...]

    def expand(which, classes):
        held = classes[...]
        for c in range(1, CLASSES):
            onehot[which, (c - 1) * 128 : c * 128, :] = jnp.where(held == BF16(c), BF16(1), BF16(0))
        onehot[which, 896:912, :] = jnp.ones((16, 2048), BF16)

    expand(0, classown)

    for copy in halo_copies:
        copy.wait_recv()
    zero = F32(0)
    lane8 = lax.broadcasted_iota(jnp.int32, (8, 128), 1)
    sub8 = lax.broadcasted_iota(jnp.int32, (8, 128), 0)
    sub8w = lax.broadcasted_iota(jnp.int32, (8, 256), 0)
    below, above = g < 15, g > 0
    right, left = s < 15, s > 0
    sides = []
    for a in range(4):
        sides.append(
            jnp.where(sub8 < 4, jnp.where(left, colin[1, a], zero), jnp.where(right, colin[0, a], zero))
        )
    columns = jnp.transpose(jnp.concatenate(sides + [jnp.zeros((96, 128), F32)], axis=0))
    for a, ref in enumerate((u_ref, up_ref, b_ref, m_ref)):
        ext[a, 0:128, 0:256] = ref[...]
        ext[a, 0:128, 256:384] = pltpu.roll(columns, 128 - (8 * a + 4), 1)
        ext[a, 128:136, 0:256] = jnp.where(
            sub8w < 4, jnp.where(below, rowin[0, a], zero), jnp.where(above, rowin[1, a], zero)
        )
        ext[a, 128:136, 256:384] = jnp.where(
            sub8 < 4,
            jnp.where(
                lane8 < 64,
                jnp.where(below & right, cornerin[0, a], zero),
                jnp.where(below & left, cornerin[1, a], zero),
            ),
            jnp.where(
                lane8 < 64,
                jnp.where(above & right, cornerin[2, a], zero),
                jnp.where(above & left, cornerin[3, a], zero),
            ),
        )
    current, previous, buoyancy, modulus = ext[0], ext[1], ext[2], ext[3]
    rows, cols = current.shape
    down = 0.5 * (modulus + pltpu.roll(modulus, rows - 1, 0))
    along = 0.5 * (modulus + pltpu.roll(modulus, cols - 1, 1))
    for step in range(STEPS):
        flux_x = down * (pltpu.roll(current, rows - 1, 0) - current)
        flux_y = along * (pltpu.roll(current, cols - 1, 1) - current)
        div = flux_x - pltpu.roll(flux_x, 1, 0) + flux_y - pltpu.roll(flux_y, 1, 1)
        following = 2.0 * current - previous + buoyancy * div
        previous, current = current, following
        block = current[0:128, 0:256]
        coarse = block.astype(BF16)
        ush[step, 0:128, :] = coarse
        ush[step, 128:256, :] = (block - coarse.astype(F32)).astype(BF16)
        if step == STEPS - 1:
            ufinal_ref[...] = block

    for copy in cell_copies:
        copy.wait_recv()
    row_at = lax.broadcasted_iota(jnp.int32, (128, 128), 0)
    col_at = lax.broadcasted_iota(jnp.int32, (256, 128), 0)
    samp_copies = [
        remote(sampsrc.at[r], sampin.at[GRID - r], samp_send.at[r], samp_recv.at[r], along_grid(r))
        for r in range(1, GRID)
    ]
    for pair in range(0, GRID, 2):
        picks, inside = [], []
        for r in (pair, pair + 1):
            cell = cells[r, 0:1, :]
            row = lax.shift_right_logical(cell, 12) - g * 128
            col = lax.bitwise_and(cell, 4095) - s * 256
            picks.append(jnp.where(col_at == col, F32(1), zero).astype(BF16))
            inside.append(row_at == row)
        found = jnp.dot(
            ush[...].reshape(4 * 256, 256), jnp.concatenate(picks, axis=1), preferred_element_type=F32
        )
        mask = jnp.concatenate(inside, axis=1)
        recorded = []
        for step in range(STEPS):
            both = found[step * 256 : step * 256 + 128] + found[step * 256 + 128 : step * 256 + 256]
            recorded.append(jnp.sum(jnp.where(mask, both, zero), axis=0, keepdims=True))
        recorded = jnp.concatenate(recorded + [jnp.zeros((4, 256), F32)], axis=0)
        sampsrc[pair] = recorded[:, 0:128]
        sampsrc[pair + 1] = recorded[:, 128:256]
        for r in (pair, pair + 1):
            if r > 0:
                samp_copies[r - 1].start()

    sib_class.wait_recv()
    expand(1, classsib)

    for slot in range(8):
        if slot == 0:
            sib_piece.wait_recv()
        else:
            dy, cross = SLOTS[slot]
            for dc in (0, 1):
                far_copies[FAR.index(((4 - dy) % 4, cross, dc))].wait_recv()
        for n in (0, 256):
            part = pl.ds(slot * SUBCHIP, SUBCHIP)
            weights = pieces[slot, :, n : n + 256]
            first = filter_ref[0:1, n : n + 256]
            total = jnp.dot(onehot[0, 896:912, part], weights, preferred_element_type=F32)
            acc = first * total[0:1]
            for c in range(1, CLASSES):
                lhs = onehot[:, (c - 1) * 128 : c * 128, part].reshape(256, SUBCHIP)
                acc = acc + (filter_ref[c : c + 1, n : n + 256] - first) * jnp.dot(
                    lhs, weights, preferred_element_type=F32
                )
            acc = acc.reshape(2, 128, 256)
            if slot == 0:
                high[:, :, n : n + 256] = acc
            else:
                high[:, :, n : n + 256] += acc

    sib_high = remote(high.at[1], highin, sib_send.at[2], sib_recv.at[2], sibling)
    sib_high.start()

    for copy in samp_copies:
        copy.wait_recv()
    samples = sampsrc[0]
    for r in range(1, GRID):
        samples = samples + sampin[r]
    across = jnp.transpose(jnp.concatenate([samples, jnp.zeros((120, 128), F32)], axis=0))
    basis = basis_ref[...]
    low = across[:, 0:1] * basis[0:1, :]
    for step in range(1, STEPS):
        low = low + across[:, step : step + 1] * basis[step : step + 1, :]
    lowpass = jnp.concatenate([cross_ref[...], cross_ref[...]], axis=1)
    weight = lowpass * (1.0 - lowpass)
    numer = jnp.sum(weight * low * low, axis=1, keepdims=True) * (1.0 / 1024)
    sib_high.wait_recv()
    mine, other = high[0], highin[...]
    full = jnp.concatenate(
        [jnp.where(core == 0, mine, other), jnp.where(core == 0, other, mine)], axis=1
    )
    denom = jnp.sum(weight * full * full, axis=1, keepdims=True) * (1.0 / 1024)
    ratio = jnp.sqrt((numer + 1e-06) / (denom + 1e-06))
    out_ref[...] = lowpass * low + (1.0 - lowpass) * (ratio * full)

    for copy in halo_copies + cell_copies + samp_copies + far_copies + [sib_piece, sib_class, sib_high]:
        copy.wait_send()


def local(
    u_now,
    u_prev,
    buoyancy,
    modulus,
    station_cell,
    path_class,
    spectra,
    cos_table,
    sin_table,
    path_filter,
    lf_basis,
    crossover,
):
    vmem = pl.BlockSpec(memory_space=pltpu.VMEM)
    dma = pltpu.SemaphoreType.DMA
    return tuple(
        pl.pallas_call(
            kernel,
            out_shape=(
                jax.ShapeDtypeStruct((128, 1024), F32),
                jax.ShapeDtypeStruct((128, 256), F32),
            ),
            in_specs=[vmem] * 12,
            out_specs=(vmem, vmem),
            scratch_shapes=[
                pltpu.VMEM((16, 8, 128), jnp.int32),
                pltpu.VMEM((8, 128), jnp.int32),
                pltpu.VMEM((2, 4, 8, 256), F32),
                pltpu.VMEM((4, 8, 128), F32),
                pltpu.VMEM((2, 4, 8, 256), F32),
                pltpu.VMEM((2, 4, 8, 128), F32),
                pltpu.VMEM((4, 4, 8, 128), F32),
                pltpu.VMEM((4, 136, 384), F32),
                pltpu.VMEM((4, 256, 256), BF16),
                pltpu.VMEM((16, 8, 128), F32),
                pltpu.VMEM((16, 8, 128), F32),
                pltpu.VMEM((128, 2048), BF16),
                pltpu.VMEM((128, 2048), BF16),
                pltpu.VMEM((2, 912, 2048), BF16),
                pltpu.VMEM((2, 128, 512), BF16),
                pltpu.VMEM((8, 256, 512), BF16),
                pltpu.VMEM((2, 128, 512), F32),
                pltpu.VMEM((128, 512), F32),
                dma((16,)),
                dma((16,)),
                dma((8,)),
                dma((8,)),
                dma((16,)),
                dma((16,)),
                dma((14,)),
                dma((14,)),
                dma((3,)),
                dma((3,)),
            ],
            compiler_params=pltpu.CompilerParams(
                collective_id=0, has_side_effects=True, vmem_limit_bytes=48 * 1024 * 1024
            ),
        )(
            u_now,
            u_prev,
            buoyancy,
            modulus,
            station_cell.reshape(1, 128),
            path_class,
            spectra,
            cos_table,
            sin_table,
            path_filter,
            lf_basis,
            crossover.reshape(1, 512),
        )
    )


def solution(mesh):
    in_specs = (
        P("grid", "sta"),
        P("grid", "sta"),
        P("grid", "sta"),
        P("grid", "sta"),
        P(("grid", "sta")),
        P(("grid", "sta"), None),
        P("sta", None),
        P("sta", None),
        P("sta", None),
        P(),
        P(),
        P(),
    )
    out_specs = (P(("grid", "sta"), None), P("grid", "sta"))
    return jax.shard_map(local, mesh=mesh, in_specs=in_specs, out_specs=out_specs, check_vma=False)
```

```python
import functools

import jax
import jax.numpy as jnp
from jax import lax
from jax.experimental import pallas as pl
from jax.experimental.pallas import tpu as pltpu
from jax.sharding import PartitionSpec as P

STEPS = 4
CLASSES = 8
MESH = pl.DeviceIdType.MESH
BF16 = jnp.bfloat16
F32 = jnp.float32

SLOTS = ((0, 0), (0, 1), (1, 0), (3, 0), (1, 1), (3, 1), (2, 0), (2, 1))
CUTS = (
    None,
    (0, 32, 48, 64),
    (0, 16, 48, 64),
    (0, 16, 32, 64),
    (0, 32, 48, 64),
    (0, 16, 48, 64),
    (0, 32, 48, 64),
    (0, 16, 32, 64),
)
SIDES = [(0, -1), (0, 1), (-1, -1), (-1, 1), (1, -1), (1, 1)]
HALO = [(-1, 0), (1, 0)] + SIDES
GRID = 16
SUBCHIP = 256


def kernel(
    u_ref,
    up_ref,
    b_ref,
    m_ref,
    cell_ref,
    class_ref,
    spectra_ref,
    cos_ref,
    sin_ref,
    filter_ref,
    basis_ref,
    cross_ref,
    out_ref,
    ufinal_ref,
    cellraw,
    classraw,
    spectra,
    cosines,
    sines,
    filters,
    bases,
    crossing,
    cells,
    cellsrc,
    colsrc,
    rowin,
    colin,
    cornerin,
    ext,
    ush,
    sampsrc,
    sampin,
    classown,
    classsib,
    onehot,
    phased,
    pieces,
    high,
    highin,
    load_sem,
    cell_send,
    cell_recv,
    halo_send,
    halo_recv,
    samp_send,
    samp_recv,
    near_send,
    near_recv,
    relay_send,
    relay_recv,
    plane_send,
    plane_recv,
    sib_send,
    sib_recv,
):
    g = lax.axis_index("grid")
    s = lax.axis_index("sta")
    z, xl = g // 2, g % 2
    y, xh, core = s // 4, (s // 2) % 2, s % 2
    colour = (z + xl) % 2

    def along_grid(r):
        return ((g + r) % GRID, s)

    def beside(dg, ds):
        return ((g + dg + 16) % 16, (s + ds + 16) % 16)

    def chip(dy, cross, dc):
        xh2 = (xh + cross) % 2
        xl2 = (xl + cross) % 2
        return (z * 2 + xl2, (((y + dy) % 4) * 2 + xh2) * 2 + (core + dc) % 2)

    sibling = chip(0, 0, 1)
    plane = [((g + 2) % 16, s), ((g + 14) % 16, s), (z * 2 + 1 - xl, s)]
    near = [(dy, cross, dc) for dy, cross in ((1, 0), (3, 0), (0, 1)) for dc in (0, 1)]
    partners = [chip(*o) for o in near] + [sibling]
    partners += [beside(*o) for o in SIDES]
    partners += [along_grid(r) for r in range(1, GRID)]
    barrier = pltpu.get_barrier_semaphore()
    for partner in partners:
        pl.semaphore_signal(barrier, inc=1, device_id=partner, device_id_type=MESH)

    def load(i, src, dst):
        copy = pltpu.make_async_copy(src, dst, load_sem.at[i])
        copy.start()
        return copy

    load_cell = load(0, cell_ref, cellraw)
    load_grid = [
        load(1 + a, ref, ext.at[a, pl.ds(0, 128), pl.ds(0, 256)])
        for a, ref in enumerate((u_ref, up_ref, b_ref, m_ref))
    ]
    load_phase = [load(5, spectra_ref, spectra), load(6, cos_ref, cosines), load(7, sin_ref, sines)]
    load_class = load(8, class_ref, classraw)
    load_rest = [load(9, filter_ref, filters), load(10, basis_ref, bases), load(11, cross_ref, crossing)]

    load_cell.wait()
    cellsrc[...] = jnp.broadcast_to(cellraw[...], (8, 128))
    lane = lax.broadcasted_iota(jnp.int32, (128, 128), 1)
    packed = jnp.zeros((128, 128), F32)
    for a in range(4):
        load_grid[a].wait()
        both = jnp.where(lane < 64, ext[a, 0:128, 0:128], ext[a, 0:128, 128:256])
        packed = jnp.where(lane // 8 == a, pltpu.roll(both, 8 * a + 4, 1), packed)
    colsrc[...] = jnp.transpose(packed)[0:32].reshape(4, 8, 128)
    for copy in load_phase:
        copy.wait()
    wide = spectra[...].astype(F32)
    phased[0] = (wide * cosines[...]).astype(BF16).reshape(2, 64, 512)
    phased[1] = (wide * sines[...]).astype(BF16).reshape(2, 64, 512)
    load_class.wait()
    for slot, (dy, cross) in enumerate(SLOTS):
        source = ((y + dy) % 4) * 2 + (xh + cross) % 2
        columns = pl.ds(pl.multiple_of(source * SUBCHIP, SUBCHIP), SUBCHIP)
        classown[:, slot * SUBCHIP : (slot + 1) * SUBCHIP] = classraw[:, columns].astype(F32).astype(BF16)

    pl.semaphore_wait(barrier, len(partners))

    def remote(src, dst, send, recv, target):
        copy = pltpu.make_async_remote_copy(
            src_ref=src, dst_ref=dst, send_sem=send, recv_sem=recv, device_id=target, device_id_type=MESH
        )
        copy.start()
        return copy

    halo_copies = []
    for i, (dg, ds) in enumerate(HALO):
        side = 1 if dg == 1 else 0
        rows = pl.ds(120 * side, 8)
        if ds == 0:
            src, dst = ext.at[:, rows, pl.ds(0, 256)], rowin.at[side]
        elif dg == 0:
            src, dst = colsrc, colin.at[1 if ds == 1 else 0]
        else:
            half = 1 if ds == 1 else 0
            src, dst = ext.at[:, rows, pl.ds(half * 128, 128)], cornerin.at[side * 2 + half]
        halo_copies.append(remote(src, dst, halo_send.at[i], halo_recv.at[i], beside(dg, ds)))
    cell_copies = [
        remote(cellsrc, cells.at[GRID - r], cell_send.at[r], cell_recv.at[r], along_grid(r)) for r in range(1, GRID)
    ]
    near_copies = []
    for i, (dy, cross, dc) in enumerate(near):
        slot = SLOTS.index(((4 - dy) % 4, cross))
        half = 1 - colour if cross else colour
        near_copies.append(
            remote(
                phased.at[(core + dc) % 2, half],
                pieces.at[slot, core, half],
                near_send.at[i],
                near_recv.at[i],
                chip(dy, cross, dc),
            )
        )
    sib_class = remote(classown, classsib, sib_send.at[1], sib_recv.at[1], sibling)
    sib_piece = remote(phased.at[1 - core], pieces.at[0, core], sib_send.at[0], sib_recv.at[0], sibling)

    relay_copies = []

    def relay(source, dy, slot, start, size):
        i = len(relay_copies)
        relay_copies.append(
            remote(
                pieces.at[source, :, colour, pl.ds(start, size)],
                pieces.at[slot, :, colour, pl.ds(start, size)],
                relay_send.at[i],
                relay_recv.at[i],
                chip(dy, 0, 0),
            )
        )

    plane_copies = {}

    def share(slot, part):
        start, stop = CUTS[slot][part], CUTS[slot][part + 1]
        rows = pieces.at[slot, :, colour, pl.ds(start, stop - start)]
        i = (slot - 1) * 3 + part
        plane_copies[slot, part] = remote(rows, rows, plane_send.at[i], plane_recv.at[i], plane[part])

    pieces[0, core] = phased[core]
    cells[0] = cellsrc[...]

    def expand(which, classes):
        held = classes[...]
        for c in range(1, CLASSES):
            onehot[which, (c - 1) * 128 : c * 128, :] = jnp.where(held == BF16(c), BF16(1), BF16(0))
        onehot[which, 896:912, :] = jnp.ones((16, 2048), BF16)

    expand(0, classown)

    for copy in halo_copies:
        copy.wait_recv()
    zero = F32(0)
    lane8 = lax.broadcasted_iota(jnp.int32, (8, 128), 1)
    sub8 = lax.broadcasted_iota(jnp.int32, (8, 128), 0)
    sub8w = lax.broadcasted_iota(jnp.int32, (8, 256), 0)
    below, above = g < 15, g > 0
    right, left = s < 15, s > 0
    sides = []
    for a in range(4):
        sides.append(
            jnp.where(sub8 < 4, jnp.where(left, colin[1, a], zero), jnp.where(right, colin[0, a], zero))
        )
    columns = jnp.transpose(jnp.concatenate(sides + [jnp.zeros((96, 128), F32)], axis=0))
    for a in range(4):
        ext[a, 0:128, 256:384] = pltpu.roll(columns, 128 - (8 * a + 4), 1)
        ext[a, 128:136, 0:256] = jnp.where(
            sub8w < 4, jnp.where(below, rowin[0, a], zero), jnp.where(above, rowin[1, a], zero)
        )
        ext[a, 128:136, 256:384] = jnp.where(
            sub8 < 4,
            jnp.where(
                lane8 < 64,
                jnp.where(below & right, cornerin[0, a], zero),
                jnp.where(below & left, cornerin[1, a], zero),
            ),
            jnp.where(
                lane8 < 64,
                jnp.where(above & right, cornerin[2, a], zero),
                jnp.where(above & left, cornerin[3, a], zero),
            ),
        )
    current, previous, buoyancy, modulus = ext[0], ext[1], ext[2], ext[3]
    rows, cols = current.shape
    down = 0.5 * (modulus + pltpu.roll(modulus, rows - 1, 0))
    along = 0.5 * (modulus + pltpu.roll(modulus, cols - 1, 1))
    for step in range(STEPS):
        flux_x = down * (pltpu.roll(current, rows - 1, 0) - current)
        flux_y = along * (pltpu.roll(current, cols - 1, 1) - current)
        div = flux_x - pltpu.roll(flux_x, 1, 0) + flux_y - pltpu.roll(flux_y, 1, 1)
        following = 2.0 * current - previous + buoyancy * div
        previous, current = current, following
        block = current[0:128, 0:256]
        coarse = block.astype(BF16)
        ush[step, 0:128, :] = coarse
        ush[step, 128:256, :] = (block - coarse.astype(F32)).astype(BF16)
        if step == STEPS - 1:
            ufinal_ref[...] = block

    for copy in near_copies:
        copy.wait_recv()
    relay(1, 1, 5, 0, 64)
    relay(1, 3, 4, 0, 64)
    relay(3, 1, 6, 0, 32)
    relay(2, 3, 6, 32, 32)
    for slot in (1, 2, 3):
        for part in range(3):
            share(slot, part)

    for copy in cell_copies:
        copy.wait_recv()
    row_at = lax.broadcasted_iota(jnp.int32, (128, 128), 0)
    col_at = lax.broadcasted_iota(jnp.int32, (256, 128), 0)
    samp_copies = []
    for pair in range(0, GRID, 2):
        picks, inside = [], []
        for r in (pair, pair + 1):
            cell = cells[r, 0:1, :]
            row = lax.shift_right_logical(cell, 12) - g * 128
            col = lax.bitwise_and(cell, 4095) - s * 256
            picks.append(jnp.where(col_at == col, F32(1), zero).astype(BF16))
            inside.append(row_at == row)
        found = jnp.dot(
            ush[...].reshape(4 * 256, 256), jnp.concatenate(picks, axis=1), preferred_element_type=F32
        )
        mask = jnp.concatenate(inside, axis=1)
        recorded = []
        for step in range(STEPS):
            both = found[step * 256 : step * 256 + 128] + found[step * 256 + 128 : step * 256 + 256]
            recorded.append(jnp.sum(jnp.where(mask, both, zero), axis=0, keepdims=True))
        recorded = jnp.concatenate(recorded + [jnp.zeros((4, 256), F32)], axis=0)
        sampsrc[pair] = recorded[:, 0:128]
        sampsrc[pair + 1] = recorded[:, 128:256]
        for r in (pair, pair + 1):
            if r > 0:
                samp_copies.append(
                    remote(sampsrc.at[r], sampin.at[GRID - r], samp_send.at[r], samp_recv.at[r], along_grid(r))
                )

    sib_class.wait_recv()
    expand(1, classsib)
    for copy in load_rest:
        copy.wait()

    def multiply(slot):
        for part in range(3) if slot else ():
            plane_copies[slot, part].wait_recv()
        part = pl.ds(slot * SUBCHIP, SUBCHIP)
        for n in (0, 256):
            weights = pieces[slot, :, :, :, n : n + 256].reshape(SUBCHIP, 256)
            first = filters[0:1, n : n + 256]
            total = jnp.dot(onehot[0, 896:912, part], weights, preferred_element_type=F32)
            acc = first * total[0:1]
            for c in range(1, CLASSES):
                lhs = onehot[:, (c - 1) * 128 : c * 128, part].reshape(256, SUBCHIP)
                acc = acc + (filters[c : c + 1, n : n + 256] - first) * jnp.dot(
                    lhs, weights, preferred_element_type=F32
                )
            acc = acc.reshape(2, 128, 256)
            if slot == 0:
                high[:, :, n : n + 256] = acc
            else:
                high[:, :, n : n + 256] += acc

    sib_piece.wait_recv()
    multiply(0)
    multiply(1)
    for copy in relay_copies[0:4]:
        copy.wait_recv()
    relay(5, 1, 7, 0, 32)
    relay(4, 3, 7, 32, 32)
    for slot in (4, 5, 6):
        for part in range(3):
            share(slot, part)
    multiply(2)
    multiply(3)
    for copy in relay_copies[4:6]:
        copy.wait_recv()
    for part in range(3):
        share(7, part)
    for slot in (4, 5, 6, 7):
        multiply(slot)

    sib_high = remote(high.at[1], highin, sib_send.at[2], sib_recv.at[2], sibling)

    for copy in samp_copies:
        copy.wait_recv()
    samples = sampsrc[0]
    for r in range(1, GRID):
        samples = samples + sampin[r]
    across = jnp.transpose(jnp.concatenate([samples, jnp.zeros((120, 128), F32)], axis=0))
    basis = bases[...]
    low = across[:, 0:1] * basis[0:1, :]
    for step in range(1, STEPS):
        low = low + across[:, step : step + 1] * basis[step : step + 1, :]
    lowpass = jnp.concatenate([crossing[...], crossing[...]], axis=1)
    weight = lowpass * (1.0 - lowpass)
    numer = jnp.sum(weight * low * low, axis=1, keepdims=True) * (1.0 / 1024)
    sib_high.wait_recv()
    mine, other = high[0], highin[...]
    full = jnp.concatenate(
        [jnp.where(core == 0, mine, other), jnp.where(core == 0, other, mine)], axis=1
    )
    denom = jnp.sum(weight * full * full, axis=1, keepdims=True) * (1.0 / 1024)
    ratio = jnp.sqrt((numer + 1e-06) / (denom + 1e-06))
    out_ref[...] = lowpass * low + (1.0 - lowpass) * (ratio * full)

    sent = halo_copies + cell_copies + samp_copies + near_copies + relay_copies + list(plane_copies.values())
    for copy in sent + [sib_piece, sib_class, sib_high]:
        copy.wait_send()


def local(
    u_now,
    u_prev,
    buoyancy,
    modulus,
    station_cell,
    path_class,
    spectra,
    cos_table,
    sin_table,
    path_filter,
    lf_basis,
    crossover,
):
    vmem = pl.BlockSpec(memory_space=pltpu.VMEM)
    dma = pltpu.SemaphoreType.DMA
    return tuple(
        pl.pallas_call(
            kernel,
            out_shape=(
                jax.ShapeDtypeStruct((128, 1024), F32),
                jax.ShapeDtypeStruct((128, 256), F32),
            ),
            in_specs=[pl.BlockSpec(memory_space=pl.ANY)] * 12,
            out_specs=(vmem, vmem),
            scratch_shapes=[
                pltpu.VMEM((1, 128), jnp.int32),
                pltpu.VMEM((128, 2048), jnp.int32),
                pltpu.VMEM((128, 512), BF16),
                pltpu.VMEM((128, 512), F32),
                pltpu.VMEM((128, 512), F32),
                pltpu.VMEM((8, 512), F32),
                pltpu.VMEM((4, 1024), F32),
                pltpu.VMEM((1, 512), F32),
                pltpu.VMEM((16, 8, 128), jnp.int32),
                pltpu.VMEM((8, 128), jnp.int32),
                pltpu.VMEM((4, 8, 128), F32),
                pltpu.VMEM((2, 4, 8, 256), F32),
                pltpu.VMEM((2, 4, 8, 128), F32),
                pltpu.VMEM((4, 4, 8, 128), F32),
                pltpu.VMEM((4, 136, 384), F32),
                pltpu.VMEM((4, 256, 256), BF16),
                pltpu.VMEM((16, 8, 128), F32),
                pltpu.VMEM((16, 8, 128), F32),
                pltpu.VMEM((128, 2048), BF16),
                pltpu.VMEM((128, 2048), BF16),
                pltpu.VMEM((2, 912, 2048), BF16),
                pltpu.VMEM((2, 2, 64, 512), BF16),
                pltpu.VMEM((8, 2, 2, 64, 512), BF16),
                pltpu.VMEM((2, 128, 512), F32),
                pltpu.VMEM((128, 512), F32),
                dma((12,)),
                dma((16,)),
                dma((16,)),
                dma((8,)),
                dma((8,)),
                dma((16,)),
                dma((16,)),
                dma((6,)),
                dma((6,)),
                dma((6,)),
                dma((6,)),
                dma((21,)),
                dma((21,)),
                dma((3,)),
                dma((3,)),
            ],
            compiler_params=pltpu.CompilerParams(
                collective_id=0, has_side_effects=True, vmem_limit_bytes=60 * 1024 * 1024
            ),
        )(
            u_now,
            u_prev,
            buoyancy,
            modulus,
            station_cell.reshape(1, 128),
            path_class,
            spectra,
            cos_table,
            sin_table,
            path_filter,
            lf_basis,
            crossover.reshape(1, 512),
        )
    )


def solution(mesh):
    in_specs = (
        P("grid", "sta"),
        P("grid", "sta"),
        P("grid", "sta"),
        P("grid", "sta"),
        P(("grid", "sta")),
        P(("grid", "sta"), None),
        P("sta", None),
        P("sta", None),
        P("sta", None),
        P(),
        P(),
        P(),
    )
    out_specs = (P(("grid", "sta"), None), P("grid", "sta"))
    return jax.shard_map(local, mesh=mesh, in_specs=in_specs, out_specs=out_specs, check_vma=False)
```

```python
import functools

import jax
import jax.numpy as jnp
from jax import lax
from jax.experimental import pallas as pl
from jax.experimental.pallas import tpu as pltpu
from jax.sharding import PartitionSpec as P

STEPS = 4
CLASSES = 8
MESH = pl.DeviceIdType.MESH
BF16 = jnp.bfloat16
F32 = jnp.float32

SLOTS = ((0, 0), (0, 1), (1, 0), (3, 0), (1, 1), (3, 1), (2, 0), (2, 1))
SIDES = [(0, -1), (0, 1), (-1, -1), (-1, 1), (1, -1), (1, 1)]
HALO = [(-1, 0), (1, 0)] + SIDES
GRID = 16
FARTHEST = (8, 9, 7, 10, 6, 11, 5, 12, 4, 13, 3, 14, 2, 15, 1, 0)
SUBCHIP = 256


def kernel(
    u_ref,
    up_ref,
    b_ref,
    m_ref,
    cell_ref,
    class_ref,
    spectra_ref,
    cos_ref,
    sin_ref,
    filter_ref,
    mine_ref,
    other_ref,
    samples_ref,
    field_ref,
    cellraw,
    classraw,
    spectra,
    cosines,
    sines,
    filters,
    final,
    total_samples,
    cells,
    cellsrc,
    colsrc,
    rowin,
    colin,
    cornerin,
    ext,
    ush,
    sampsrc,
    sampin,
    classown,
    classsib,
    onehot,
    phased,
    pieces,
    high,
    load_sem,
    cell_send,
    cell_recv,
    halo_send,
    halo_recv,
    samp_send,
    samp_recv,
    near_send,
    near_recv,
    relay_send,
    relay_recv,
    plane_send,
    plane_recv,
    sib_send,
    sib_recv,
):
    g = lax.axis_index("grid")
    s = lax.axis_index("sta")
    z, xl = g // 2, g % 2
    y, xh, core = s // 4, (s // 2) % 2, s % 2
    colour = (z + xl) % 2

    def along_grid(r):
        return ((g + r) % GRID, s)

    def beside(dg, ds):
        return ((g + dg + 16) % 16, (s + ds + 16) % 16)

    def chip(dy, cross, dc):
        xh2 = (xh + cross) % 2
        xl2 = (xl + cross) % 2
        return (z * 2 + xl2, (((y + dy) % 4) * 2 + xh2) * 2 + (core + dc) % 2)

    sibling = chip(0, 0, 1)
    plane = [((g + 2) % 16, s), ((g + 14) % 16, s), (z * 2 + 1 - xl, s)]
    near = [(dy, cross, dc) for dy, cross in ((1, 0), (3, 0), (0, 1)) for dc in (0, 1)]
    partners = [chip(*o) for o in near] + [sibling]
    partners += [beside(*o) for o in SIDES]
    partners += [along_grid(r) for r in range(1, GRID)]
    barrier = pltpu.get_barrier_semaphore()
    for partner in partners:
        pl.semaphore_signal(barrier, inc=1, device_id=partner, device_id_type=MESH)

    def load(i, src, dst):
        copy = pltpu.make_async_copy(src, dst, load_sem.at[i])
        copy.start()
        return copy

    load_cell = load(0, cell_ref, cellraw)
    load_phase = [load(5, spectra_ref, spectra), load(6, cos_ref, cosines), load(7, sin_ref, sines)]
    load_grid = [
        load(1 + a, ref, ext.at[a, pl.ds(0, 128), pl.ds(0, 256)])
        for a, ref in enumerate((u_ref, up_ref, b_ref, m_ref))
    ]
    load_class = load(8, class_ref, classraw)
    load_filter = load(9, filter_ref, filters)

    load_cell.wait()
    cellsrc[...] = jnp.broadcast_to(cellraw[...], (8, 128))
    for copy in load_phase:
        copy.wait()
    wide = spectra[...].astype(F32)
    phased[0] = (wide * cosines[...]).astype(BF16).reshape(2, 64, 512)
    phased[1] = (wide * sines[...]).astype(BF16).reshape(2, 64, 512)
    lane = lax.broadcasted_iota(jnp.int32, (128, 128), 1)
    packed = jnp.zeros((128, 128), F32)
    for a in range(4):
        load_grid[a].wait()
        both = jnp.where(lane < 64, ext[a, 0:128, 0:128], ext[a, 0:128, 128:256])
        packed = jnp.where(lane // 8 == a, pltpu.roll(both, 8 * a + 4, 1), packed)
    colsrc[...] = jnp.transpose(packed)[0:32].reshape(4, 8, 128)

    pl.semaphore_wait(barrier, len(partners))

    def remote(src, dst, send, recv, target):
        copy = pltpu.make_async_remote_copy(
            src_ref=src, dst_ref=dst, send_sem=send, recv_sem=recv, device_id=target, device_id_type=MESH
        )
        copy.start()
        return copy

    halo_copies = []
    for i, (dg, ds) in enumerate(HALO):
        side = 1 if dg == 1 else 0
        rows = pl.ds(120 * side, 8)
        if ds == 0:
            src, dst = ext.at[:, rows, pl.ds(0, 256)], rowin.at[side]
        elif dg == 0:
            src, dst = colsrc, colin.at[1 if ds == 1 else 0]
        else:
            half = 1 if ds == 1 else 0
            src, dst = ext.at[:, rows, pl.ds(half * 128, 128)], cornerin.at[side * 2 + half]
        halo_copies.append(remote(src, dst, halo_send.at[i], halo_recv.at[i], beside(dg, ds)))
    cell_copies = [
        remote(cellsrc, cells.at[GRID - r], cell_send.at[r], cell_recv.at[r], along_grid(r)) for r in FARTHEST if r
    ]
    near_copies = {}

    def send_near(turn):
        for i, (dy, cross, dc) in enumerate(near):
            slot = SLOTS.index(((4 - dy) % 4, cross))
            half = 1 - colour if cross else colour
            part = 1 - turn if dy == 3 else turn
            rows = pl.ds(32 * part, 32)
            near_copies[dy, cross, dc, part] = remote(
                phased.at[(core + dc) % 2, half, rows],
                pieces.at[slot, core, half, rows],
                near_send.at[2 * i + part],
                near_recv.at[2 * i + part],
                chip(dy, cross, dc),
            )

    send_near(0)
    sib_piece = remote(phased.at[1 - core], pieces.at[0, core], sib_send.at[0], sib_recv.at[0], sibling)

    relay_copies = {}

    def relay(source, dy, cross, slot, part):
        i = len(relay_copies)
        rows = pl.ds(32 * part, 32)
        relay_copies[slot, cross, part] = remote(
            pieces.at[source, :, colour, rows],
            pieces.at[slot, :, colour, rows],
            relay_send.at[i],
            relay_recv.at[i],
            chip(dy, cross, 0),
        )

    plane_copies = {}

    def share(slot, part, half):
        for quarter in (2 * part, 2 * part + 1):
            rows = pieces.at[slot, :, half, pl.ds(16 * quarter, 16)]
            i = (slot - 1) * 4 + quarter
            plane_copies[slot, quarter] = remote(rows, rows, plane_send.at[i], plane_recv.at[i], plane[i % 3])

    load_class.wait()
    for slot, (dy, cross) in enumerate(SLOTS):
        source = ((y + dy) % 4) * 2 + (xh + cross) % 2
        columns = pl.ds(pl.multiple_of(source * SUBCHIP, SUBCHIP), SUBCHIP)
        classown[:, slot * SUBCHIP : (slot + 1) * SUBCHIP] = classraw[:, columns].astype(F32).astype(BF16)
    sib_class = remote(classown, classsib, sib_send.at[1], sib_recv.at[1], sibling)
    pieces[0, core] = phased[core]
    cells[0] = cellsrc[...]

    def expand(which, classes):
        held = classes[...]
        for c in range(1, CLASSES):
            onehot[which, (c - 1) * 128 : c * 128, :] = jnp.where(held == BF16(c), BF16(1), BF16(0))
        onehot[which, 896:912, :] = jnp.ones((16, 2048), BF16)

    expand(0, classown)
    send_near(1)
    sib_class.wait_recv()
    expand(1, classsib)
    load_filter.wait()

    def multiply(slot):
        for quarter in range(4) if 0 < slot < 7 else ():
            plane_copies[slot, quarter].wait_recv()
        part = pl.ds(slot * SUBCHIP, SUBCHIP)
        for n in (0, 256):
            weights = pieces[slot, :, :, :, n : n + 256].reshape(SUBCHIP, 256)
            first = filters[0:1, n : n + 256]
            total = jnp.dot(onehot[0, 896:912, part], weights, preferred_element_type=F32)
            acc = first * total[0:1]
            for c in range(1, CLASSES):
                lhs = onehot[:, (c - 1) * 128 : c * 128, part].reshape(256, SUBCHIP)
                acc = acc + (filters[c : c + 1, n : n + 256] - first) * jnp.dot(
                    lhs, weights, preferred_element_type=F32
                )
            acc = acc.reshape(2, 128, 256)
            if slot == 0:
                high[:, :, n : n + 256] = acc
            else:
                high[:, :, n : n + 256] += acc

    sib_piece.wait_recv()
    multiply(0)

    for copy in halo_copies:
        copy.wait_recv()
    zero = F32(0)
    lane8 = lax.broadcasted_iota(jnp.int32, (8, 128), 1)
    sub8 = lax.broadcasted_iota(jnp.int32, (8, 128), 0)
    sub8w = lax.broadcasted_iota(jnp.int32, (8, 256), 0)
    below, above = g < 15, g > 0
    right, left = s < 15, s > 0
    sides = []
    for a in range(4):
        sides.append(
            jnp.where(sub8 < 4, jnp.where(left, colin[1, a], zero), jnp.where(right, colin[0, a], zero))
        )
    columns = jnp.transpose(jnp.concatenate(sides + [jnp.zeros((96, 128), F32)], axis=0))
    for a in range(4):
        ext[a, 0:128, 256:384] = pltpu.roll(columns, 128 - (8 * a + 4), 1)
        ext[a, 128:136, 0:256] = jnp.where(
            sub8w < 4, jnp.where(below, rowin[0, a], zero), jnp.where(above, rowin[1, a], zero)
        )
        ext[a, 128:136, 256:384] = jnp.where(
            sub8 < 4,
            jnp.where(
                lane8 < 64,
                jnp.where(below & right, cornerin[0, a], zero),
                jnp.where(below & left, cornerin[1, a], zero),
            ),
            jnp.where(
                lane8 < 64,
                jnp.where(above & right, cornerin[2, a], zero),
                jnp.where(above & left, cornerin[3, a], zero),
            ),
        )
    current, previous, buoyancy, modulus = ext[0], ext[1], ext[2], ext[3]
    rows, cols = current.shape
    down = 0.5 * (modulus + pltpu.roll(modulus, rows - 1, 0))
    along = 0.5 * (modulus + pltpu.roll(modulus, cols - 1, 1))
    for step in range(STEPS):
        flux_x = down * (pltpu.roll(current, rows - 1, 0) - current)
        flux_y = along * (pltpu.roll(current, cols - 1, 1) - current)
        div = flux_x - pltpu.roll(flux_x, 1, 0) + flux_y - pltpu.roll(flux_y, 1, 1)
        following = 2.0 * current - previous + buoyancy * div
        previous, current = current, following
        block = current[0:128, 0:256]
        coarse = block.astype(BF16)
        ush[step, 0:128, :] = coarse
        ush[step, 128:256, :] = (block - coarse.astype(F32)).astype(BF16)
        if step == STEPS - 1:
            final[...] = block

    field_out = pltpu.make_async_copy(final, field_ref, load_sem.at[13])
    field_out.start()

    def arrived(dy, cross, part):
        for dc in (0, 1):
            near_copies[dy, cross, dc, part].wait_recv()

    for copy in ((1, 0, 0), (3, 0, 1), (0, 1, 0)):
        arrived(*copy)
    relay(3, 1, 0, 6, 0)
    relay(2, 3, 0, 6, 1)
    share(3, 0, colour)
    share(2, 1, colour)
    share(1, 0, colour)
    for copy in ((1, 0, 1), (3, 0, 0), (0, 1, 1)):
        arrived(*copy)
    relay(1, 1, 0, 5, 0)
    relay(1, 3, 0, 4, 1)
    relay(3, 0, 1, 5, 1)
    relay(2, 0, 1, 4, 0)
    share(1, 1, colour)
    share(3, 1, colour)
    share(2, 0, colour)

    for copy in cell_copies:
        copy.wait_recv()
    row_at = lax.broadcasted_iota(jnp.int32, (128, 128), 0)
    col_at = lax.broadcasted_iota(jnp.int32, (256, 128), 0)
    samp_copies = []
    for pair in range(0, GRID, 2):
        pair = FARTHEST[pair : pair + 2]
        picks, inside = [], []
        for r in pair:
            cell = cells[r, 0:1, :]
            row = lax.shift_right_logical(cell, 12) - g * 128
            col = lax.bitwise_and(cell, 4095) - s * 256
            picks.append(jnp.where(col_at == col, F32(1), zero).astype(BF16))
            inside.append(row_at == row)
        found = jnp.dot(
            ush[...].reshape(4 * 256, 256), jnp.concatenate(picks, axis=1), preferred_element_type=F32
        )
        mask = jnp.concatenate(inside, axis=1)
        recorded = []
        for step in range(STEPS):
            both = found[step * 256 : step * 256 + 128] + found[step * 256 + 128 : step * 256 + 256]
            recorded.append(jnp.sum(jnp.where(mask, both, zero), axis=0, keepdims=True))
        recorded = jnp.concatenate(recorded + [jnp.zeros((4, 256), F32)], axis=0)
        sampsrc[pair[0]] = recorded[:, 0:128]
        sampsrc[pair[1]] = recorded[:, 128:256]
        for r in pair:
            if r > 0:
                samp_copies.append(
                    remote(sampsrc.at[r], sampin.at[GRID - r], samp_send.at[r], samp_recv.at[r], along_grid(r))
                )

    relay_copies[6, 0, 0].wait_recv()
    relay_copies[6, 0, 1].wait_recv()
    relay(6, 0, 1, 7, 0)
    relay(6, 0, 1, 7, 1)
    share(6, 0, colour)
    share(6, 1, colour)
    relay_copies[5, 0, 0].wait_recv()
    relay(5, 1, 0, 7, 0)
    relay_copies[4, 0, 1].wait_recv()
    relay(4, 3, 0, 7, 1)
    share(5, 0, colour)
    share(4, 1, colour)
    multiply(1)
    relay_copies[5, 1, 1].wait_recv()
    relay_copies[4, 1, 0].wait_recv()
    share(5, 1, 1 - colour)
    share(4, 0, 1 - colour)
    for slot in (2, 3, 6):
        multiply(slot)
    for cross in (0, 1):
        for part in (0, 1):
            relay_copies[7, cross, part].wait_recv()
    multiply(7)
    multiply(4)
    multiply(5)

    sib_high = remote(high.at[1], other_ref, sib_send.at[2], sib_recv.at[2], sibling)
    mine_out = pltpu.make_async_copy(high.at[0], mine_ref, load_sem.at[12])
    mine_out.start()
    for copy in samp_copies:
        copy.wait_recv()
    samples = sampsrc[0]
    for r in range(1, GRID):
        samples = samples + sampin[r]
    total_samples[...] = samples
    samples_out = pltpu.make_async_copy(total_samples, samples_ref, load_sem.at[14])
    samples_out.start()
    sib_high.wait_recv()
    mine_out.wait()
    samples_out.wait()
    field_out.wait()

    sent = halo_copies + cell_copies + samp_copies + list(near_copies.values()) + list(relay_copies.values())
    sent += list(plane_copies.values())
    for copy in sent + [sib_piece, sib_class, sib_high]:
        copy.wait_send()


def merge(
    mine_ref,
    other_ref,
    samples_ref,
    field_ref,
    basis_ref,
    cross_ref,
    out_ref,
    ufinal_ref,
    halves,
    samples,
    bases,
    crossing,
    out,
    field,
    sem,
):
    core = lax.axis_index("sta") % 2
    field_in = pltpu.make_async_copy(field_ref, field, sem.at[0])
    field_out = pltpu.make_async_copy(field, ufinal_ref, sem.at[7])
    loads = [
        pltpu.make_async_copy(samples_ref, samples, sem.at[1]),
        pltpu.make_async_copy(basis_ref, bases, sem.at[2]),
        pltpu.make_async_copy(cross_ref, crossing, sem.at[3]),
    ]
    halves_in = [
        pltpu.make_async_copy(mine_ref, halves.at[core], sem.at[4]),
        pltpu.make_async_copy(other_ref, halves.at[1 - core], sem.at[5]),
    ]
    for copy in loads:
        copy.start()
    for copy in halves_in:
        copy.start()
    field_in.start()
    for copy in loads:
        copy.wait()
    across = jnp.transpose(jnp.concatenate([samples[...], jnp.zeros((120, 128), F32)], axis=0))
    basis = bases[...]
    lowpass = jnp.concatenate([crossing[...], crossing[...]], axis=1)
    weight = lowpass * (1.0 - lowpass)
    low = across[:, 0:1] * basis[0:1, :]
    for step in range(1, STEPS):
        low = low + across[:, step : step + 1] * basis[step : step + 1, :]
    numer = jnp.sum(weight * low * low, axis=1, keepdims=True) * (1.0 / 1024)
    field_in.wait()
    field_out.start()
    for copy in halves_in:
        copy.wait()
    full = jnp.concatenate([halves[0], halves[1]], axis=1)
    denom = jnp.sum(weight * full * full, axis=1, keepdims=True) * (1.0 / 1024)
    ratio = jnp.sqrt((numer + 1e-06) / (denom + 1e-06))
    out[...] = lowpass * low + (1.0 - lowpass) * (ratio * full)
    store = pltpu.make_async_copy(out, out_ref, sem.at[6])
    store.start()
    field_out.wait()
    store.wait()


def local(
    u_now,
    u_prev,
    buoyancy,
    modulus,
    station_cell,
    path_class,
    spectra,
    cos_table,
    sin_table,
    path_filter,
    lf_basis,
    crossover,
):
    dma = pltpu.SemaphoreType.DMA
    anywhere = pl.BlockSpec(memory_space=pl.ANY)
    mine, other, samples, field = pl.pallas_call(
            kernel,
            out_shape=(
                jax.ShapeDtypeStruct((128, 512), F32),
                jax.ShapeDtypeStruct((128, 512), F32),
                jax.ShapeDtypeStruct((8, 128), F32),
                jax.ShapeDtypeStruct((128, 256), F32),
            ),
            in_specs=[anywhere] * 10,
            out_specs=(anywhere,) * 4,
            scratch_shapes=[
                pltpu.VMEM((1, 128), jnp.int32),
                pltpu.VMEM((128, 2048), jnp.int32),
                pltpu.VMEM((128, 512), BF16),
                pltpu.VMEM((128, 512), F32),
                pltpu.VMEM((128, 512), F32),
                pltpu.VMEM((8, 512), F32),
                pltpu.VMEM((128, 256), F32),
                pltpu.VMEM((8, 128), F32),
                pltpu.VMEM((16, 8, 128), jnp.int32),
                pltpu.VMEM((8, 128), jnp.int32),
                pltpu.VMEM((4, 8, 128), F32),
                pltpu.VMEM((2, 4, 8, 256), F32),
                pltpu.VMEM((2, 4, 8, 128), F32),
                pltpu.VMEM((4, 4, 8, 128), F32),
                pltpu.VMEM((4, 136, 384), F32),
                pltpu.VMEM((4, 256, 256), BF16),
                pltpu.VMEM((16, 8, 128), F32),
                pltpu.VMEM((16, 8, 128), F32),
                pltpu.VMEM((128, 2048), BF16),
                pltpu.VMEM((128, 2048), BF16),
                pltpu.VMEM((2, 912, 2048), BF16),
                pltpu.VMEM((2, 2, 64, 512), BF16),
                pltpu.VMEM((8, 2, 2, 64, 512), BF16),
                pltpu.VMEM((2, 128, 512), F32),
                dma((15,)),
                dma((16,)),
                dma((16,)),
                dma((8,)),
                dma((8,)),
                dma((16,)),
                dma((16,)),
                dma((12,)),
                dma((12,)),
                dma((10,)),
                dma((10,)),
                dma((28,)),
                dma((28,)),
                dma((3,)),
                dma((3,)),
            ],
            compiler_params=pltpu.CompilerParams(
                collective_id=0, has_side_effects=True, vmem_limit_bytes=60 * 1024 * 1024
            ),
        )(
            u_now,
            u_prev,
            buoyancy,
            modulus,
            station_cell.reshape(1, 128),
            path_class,
            spectra,
            cos_table,
            sin_table,
            path_filter,
    )
    return pl.pallas_call(
        merge,
        out_shape=(jax.ShapeDtypeStruct((128, 1024), F32), jax.ShapeDtypeStruct((128, 256), F32)),
        in_specs=[anywhere] * 6,
        out_specs=(anywhere,) * 2,
        scratch_shapes=[
            pltpu.VMEM((2, 128, 512), F32),
            pltpu.VMEM((8, 128), F32),
            pltpu.VMEM((4, 1024), F32),
            pltpu.VMEM((1, 512), F32),
            pltpu.VMEM((128, 1024), F32),
            pltpu.VMEM((128, 256), F32),
            dma((8,)),
        ],
        compiler_params=pltpu.CompilerParams(vmem_limit_bytes=60 * 1024 * 1024),
    )(mine, other, samples, field, lf_basis, crossover.reshape(1, 512))


def solution(mesh):
    in_specs = (
        P("grid", "sta"),
        P("grid", "sta"),
        P("grid", "sta"),
        P("grid", "sta"),
        P(("grid", "sta")),
        P(("grid", "sta"), None),
        P("sta", None),
        P("sta", None),
        P("sta", None),
        P(),
        P(),
        P(),
    )
    out_specs = (P(("grid", "sta"), None), P("grid", "sta"))
    return jax.shard_map(local, mesh=mesh, in_specs=in_specs, out_specs=out_specs, check_vma=False)
```

```python
import functools

import jax
import jax.numpy as jnp
from jax import lax
from jax.experimental import pallas as pl
from jax.experimental.pallas import tpu as pltpu
from jax.sharding import PartitionSpec as P

STEPS = 4
CLASSES = 8
MESH = pl.DeviceIdType.MESH
BF16 = jnp.bfloat16
F32 = jnp.float32

SLOTS = ((0, 0), (0, 1), (1, 0), (3, 0), (1, 1), (3, 1), (2, 0), (2, 1))
SIDES = [(0, -1), (0, 1), (-1, -1), (-1, 1), (1, -1), (1, 1)]
HALO = [(-1, 0), (1, 0)] + SIDES
FORWARDED = ((6, 0, 0), (6, 0, 1), (5, 0, 0), (4, 0, 1))
GRID = 16
FARTHEST = (8, 9, 7, 10, 6, 11, 5, 12, 4, 13, 3, 14, 2, 15, 1, 0)
SUBCHIP = 256


def kernel(
    u_ref,
    up_ref,
    b_ref,
    m_ref,
    cell_ref,
    class_ref,
    spectra_ref,
    cos_ref,
    sin_ref,
    filter_ref,
    mine_ref,
    other_ref,
    samples_ref,
    field_ref,
    cellraw,
    classraw,
    spectra,
    cosines,
    sines,
    filters,
    final,
    total_samples,
    cells,
    cellsrc,
    colsrc,
    rowin,
    colin,
    cornerin,
    ext,
    ush,
    sampsrc,
    sampin,
    classown,
    classsib,
    onehot,
    phased,
    pieces,
    high,
    load_sem,
    cell_send,
    cell_recv,
    halo_send,
    halo_recv,
    samp_send,
    samp_recv,
    near_send,
    near_recv,
    relay_send,
    relay_recv,
    plane_send,
    plane_recv,
    sib_send,
    sib_recv,
):
    g = lax.axis_index("grid")
    s = lax.axis_index("sta")
    z, xl = g // 2, g % 2
    y, xh, core = s // 4, (s // 2) % 2, s % 2
    colour = (z + xl) % 2

    def along_grid(r):
        return ((g + r) % GRID, s)

    def beside(dg, ds):
        return ((g + dg + 16) % 16, (s + ds + 16) % 16)

    def chip(dy, cross, dc):
        xh2 = (xh + cross) % 2
        xl2 = (xl + cross) % 2
        return (z * 2 + xl2, (((y + dy) % 4) * 2 + xh2) * 2 + (core + dc) % 2)

    sibling = chip(0, 0, 1)
    plane = [((g + 2) % 16, s), ((g + 14) % 16, s), (z * 2 + 1 - xl, s)]
    near = [(dy, cross, dc) for dy, cross in ((1, 0), (3, 0), (0, 1)) for dc in (0, 1)]
    partners = [chip(*o) for o in near] + [sibling]
    partners += [beside(*o) for o in SIDES]
    partners += [along_grid(r) for r in range(1, GRID)]
    barrier = pltpu.get_barrier_semaphore()
    for partner in partners:
        pl.semaphore_signal(barrier, inc=1, device_id=partner, device_id_type=MESH)

    def load(i, src, dst):
        copy = pltpu.make_async_copy(src, dst, load_sem.at[i])
        copy.start()
        return copy

    load_cell = load(0, cell_ref, cellraw)
    load_phase = [load(5, spectra_ref, spectra), load(6, cos_ref, cosines), load(7, sin_ref, sines)]
    load_grid = [
        load(1 + a, ref, ext.at[a, pl.ds(0, 128), pl.ds(0, 256)])
        for a, ref in enumerate((u_ref, up_ref, b_ref, m_ref))
    ]
    load_class = load(8, class_ref, classraw)
    load_filter = load(9, filter_ref, filters)

    load_cell.wait()
    cellsrc[...] = jnp.broadcast_to(cellraw[...], (8, 128))
    for copy in load_phase:
        copy.wait()
    wide = spectra[...].astype(F32)
    phased[0] = (wide * cosines[...]).astype(BF16).reshape(2, 64, 512)
    phased[1] = (wide * sines[...]).astype(BF16).reshape(2, 64, 512)
    lane = lax.broadcasted_iota(jnp.int32, (128, 128), 1)
    packed = jnp.zeros((128, 128), F32)
    for a in range(4):
        load_grid[a].wait()
        both = jnp.where(lane < 64, ext[a, 0:128, 0:128], ext[a, 0:128, 128:256])
        packed = jnp.where(lane // 8 == a, pltpu.roll(both, 8 * a + 4, 1), packed)
    colsrc[...] = jnp.transpose(packed)[0:32].reshape(4, 8, 128)

    load_class.wait()
    for slot, (dy, cross) in enumerate(SLOTS):
        source = ((y + dy) % 4) * 2 + (xh + cross) % 2
        columns = pl.ds(pl.multiple_of(source * SUBCHIP, SUBCHIP), SUBCHIP)
        classown[:, slot * SUBCHIP : (slot + 1) * SUBCHIP] = classraw[:, columns].astype(F32).astype(BF16)
    def expand(which, classes):
        held = classes[...]
        for c in range(1, CLASSES):
            onehot[which, (c - 1) * 128 : c * 128, :] = jnp.where(held == BF16(c), BF16(1), BF16(0))
        onehot[which, 896:912, :] = jnp.ones((16, 2048), BF16)

    expand(0, classown)

    pl.semaphore_wait(barrier, len(partners))

    def remote(src, dst, send, recv, target):
        copy = pltpu.make_async_remote_copy(
            src_ref=src, dst_ref=dst, send_sem=send, recv_sem=recv, device_id=target, device_id_type=MESH
        )
        copy.start()
        return copy

    halo_copies = []
    for i, (dg, ds) in enumerate(HALO):
        side = 1 if dg == 1 else 0
        rows = pl.ds(120 * side, 8)
        if ds == 0:
            src, dst = ext.at[:, rows, pl.ds(0, 256)], rowin.at[side]
        elif dg == 0:
            src, dst = colsrc, colin.at[1 if ds == 1 else 0]
        else:
            half = 1 if ds == 1 else 0
            src, dst = ext.at[:, rows, pl.ds(half * 128, 128)], cornerin.at[side * 2 + half]
        halo_copies.append(remote(src, dst, halo_send.at[i], halo_recv.at[i], beside(dg, ds)))
    cell_copies = {
        GRID - r: remote(cellsrc, cells.at[GRID - r], cell_send.at[r], cell_recv.at[r], along_grid(r))
        for r in FARTHEST
        if r
    }
    near_copies = {}

    def send_near(turn):
        for i, (dy, cross, dc) in enumerate(near):
            slot = SLOTS.index(((4 - dy) % 4, cross))
            half = 1 - colour if cross else colour
            part = 1 - turn if dy == 3 else turn
            rows = pl.ds(32 * part, 32)
            near_copies[dy, cross, dc, part] = remote(
                phased.at[(core + dc) % 2, half, rows],
                pieces.at[slot, core, half, rows],
                near_send.at[2 * i + part],
                near_recv.at[2 * i + part],
                chip(dy, cross, dc),
            )

    send_near(0)
    sib_piece = remote(phased.at[1 - core], pieces.at[0, core], sib_send.at[0], sib_recv.at[0], sibling)

    relay_copies = {}

    def relay(source, dy, cross, slot, part):
        i = len(relay_copies)
        rows = pl.ds(32 * part, 32)
        relay_copies[slot, cross, part] = remote(
            pieces.at[source, :, colour, rows],
            pieces.at[slot, :, colour, rows],
            relay_send.at[i],
            relay_recv.at[i],
            chip(dy, cross, 0),
        )

    plane_copies = {}

    def share(slot, part, half):
        for quarter in (2 * part, 2 * part + 1):
            rows = pieces.at[slot, :, half, pl.ds(16 * quarter, 16)]
            i = (slot - 1) * 4 + quarter
            plane_copies[slot, quarter] = remote(rows, rows, plane_send.at[i], plane_recv.at[i], plane[i % 3])

    sib_class = remote(classown, classsib, sib_send.at[1], sib_recv.at[1], sibling)
    pieces[0, core] = phased[core]
    cells[0] = cellsrc[...]

    sib_piece.wait_recv()
    send_near(1)
    sib_class.wait_recv()
    expand(1, classsib)
    load_filter.wait()

    def arrived(dy, cross, part):
        for dc in (0, 1):
            near_copies[dy, cross, dc, part].wait_recv()

    for copy in ((1, 0, 0), (3, 0, 1), (0, 1, 0)):
        arrived(*copy)
    relay(3, 1, 0, 6, 0)
    relay(2, 3, 0, 6, 1)
    share(3, 0, colour)
    share(2, 1, colour)
    share(1, 0, colour)

    for copy in halo_copies:
        copy.wait_recv()
    zero = F32(0)
    lane8 = lax.broadcasted_iota(jnp.int32, (8, 128), 1)
    sub8 = lax.broadcasted_iota(jnp.int32, (8, 128), 0)
    sub8w = lax.broadcasted_iota(jnp.int32, (8, 256), 0)
    below, above = g < 15, g > 0
    right, left = s < 15, s > 0
    sides = []
    for a in range(4):
        sides.append(
            jnp.where(sub8 < 4, jnp.where(left, colin[1, a], zero), jnp.where(right, colin[0, a], zero))
        )
    columns = jnp.transpose(jnp.concatenate(sides + [jnp.zeros((96, 128), F32)], axis=0))
    for a in range(4):
        ext[a, 0:128, 256:384] = pltpu.roll(columns, 128 - (8 * a + 4), 1)
        ext[a, 128:136, 0:256] = jnp.where(
            sub8w < 4, jnp.where(below, rowin[0, a], zero), jnp.where(above, rowin[1, a], zero)
        )
        ext[a, 128:136, 256:384] = jnp.where(
            sub8 < 4,
            jnp.where(
                lane8 < 64,
                jnp.where(below & right, cornerin[0, a], zero),
                jnp.where(below & left, cornerin[1, a], zero),
            ),
            jnp.where(
                lane8 < 64,
                jnp.where(above & right, cornerin[2, a], zero),
                jnp.where(above & left, cornerin[3, a], zero),
            ),
        )
    current, previous, buoyancy, modulus = ext[0], ext[1], ext[2], ext[3]
    rows, cols = current.shape
    down = 0.5 * (modulus + pltpu.roll(modulus, rows - 1, 0))
    along = 0.5 * (modulus + pltpu.roll(modulus, cols - 1, 1))
    for step in range(STEPS):
        flux_x = down * (pltpu.roll(current, rows - 1, 0) - current)
        flux_y = along * (pltpu.roll(current, cols - 1, 1) - current)
        div = flux_x - pltpu.roll(flux_x, 1, 0) + flux_y - pltpu.roll(flux_y, 1, 1)
        following = 2.0 * current - previous + buoyancy * div
        previous, current = current, following
        block = current[0:128, 0:256]
        coarse = block.astype(BF16)
        ush[step, 0:128, :] = coarse
        ush[step, 128:256, :] = (block - coarse.astype(F32)).astype(BF16)
        if step == STEPS - 1:
            final[...] = block

    field_out = pltpu.make_async_copy(final, field_ref, load_sem.at[13])
    field_out.start()

    for copy in ((1, 0, 1), (3, 0, 0), (0, 1, 1)):
        arrived(*copy)
    relay(1, 1, 0, 5, 0)
    relay(1, 3, 0, 4, 1)
    relay(3, 0, 1, 5, 1)
    relay(2, 0, 1, 4, 0)
    share(1, 1, colour)
    share(3, 1, colour)
    share(2, 0, colour)

    results, stores = [], []

    def multiply(slot):
        for quarter in range(4):
            if (slot, quarter) in plane_copies:
                plane_copies[slot, quarter].wait_recv()
        for cross, part in ((0, 0), (0, 1), (1, 0), (1, 1)):
            if (slot, cross, part) in relay_copies and (slot, cross, part) not in FORWARDED:
                relay_copies[slot, cross, part].wait_recv()
        part = pl.ds(slot * SUBCHIP, SUBCHIP)
        for n in (0, 256):
            weights = pieces[slot, :, :, :, n : n + 256].reshape(SUBCHIP, 256)
            first = filters[0:1, n : n + 256]
            total = jnp.dot(onehot[0, 896:912, part], weights, preferred_element_type=F32)
            acc = first * total[0:1]
            for c in range(1, CLASSES):
                lhs = onehot[:, (c - 1) * 128 : c * 128, part].reshape(256, SUBCHIP)
                acc = acc + (filters[c : c + 1, n : n + 256] - first) * jnp.dot(
                    lhs, weights, preferred_element_type=F32
                )
            acc = acc.reshape(2, 128, 256)
            if slot == 0:
                high[:, :, n : n + 256] = acc
            else:
                high[:, :, n : n + 256] += acc
            if slot == 7:
                done = pl.ds(n, 256)
                i = 2 + n // 256
                results.append(
                    remote(high.at[1, :, done], other_ref.at[:, done], sib_send.at[i], sib_recv.at[i], sibling)
                )
                mine_out = pltpu.make_async_copy(high.at[0, :, done], mine_ref.at[:, done], load_sem.at[13 + i])
                mine_out.start()
                stores.append(mine_out)

    row_at = lax.broadcasted_iota(jnp.int32, (128, 128), 0)
    col_at = lax.broadcasted_iota(jnp.int32, (256, 128), 0)
    samp_copies = []
    for pair in range(0, GRID, 2):
        pair = FARTHEST[14 - pair : 16 - pair]
        for r in pair:
            if r > 0:
                cell_copies[r].wait_recv()
        picks, inside = [], []
        for r in pair:
            cell = cells[r, 0:1, :]
            row = lax.shift_right_logical(cell, 12) - g * 128
            col = lax.bitwise_and(cell, 4095) - s * 256
            picks.append(jnp.where(col_at == col, F32(1), zero).astype(BF16))
            inside.append(row_at == row)
        found = jnp.dot(
            ush[...].reshape(4 * 256, 256), jnp.concatenate(picks, axis=1), preferred_element_type=F32
        )
        mask = jnp.concatenate(inside, axis=1)
        recorded = []
        for step in range(STEPS):
            both = found[step * 256 : step * 256 + 128] + found[step * 256 + 128 : step * 256 + 256]
            recorded.append(jnp.sum(jnp.where(mask, both, zero), axis=0, keepdims=True))
        recorded = jnp.concatenate(recorded + [jnp.zeros((4, 256), F32)], axis=0)
        sampsrc[pair[0]] = recorded[:, 0:128]
        sampsrc[pair[1]] = recorded[:, 128:256]
        for r in pair:
            if r > 0:
                samp_copies.append(
                    remote(sampsrc.at[r], sampin.at[GRID - r], samp_send.at[r], samp_recv.at[r], along_grid(r))
                )

    relay(1, 1, 0, 5, 1)
    relay(1, 3, 0, 4, 0)
    multiply(0)
    relay_copies[6, 0, 0].wait_recv()
    relay_copies[6, 0, 1].wait_recv()
    relay(6, 0, 1, 7, 0)
    relay(6, 0, 1, 7, 1)
    share(6, 0, colour)
    share(6, 1, colour)
    relay_copies[5, 0, 0].wait_recv()
    relay(5, 1, 0, 7, 0)
    relay_copies[4, 0, 1].wait_recv()
    relay(4, 3, 0, 7, 1)
    share(5, 0, colour)
    share(4, 1, colour)
    for slot in (1, 2, 3, 6, 5, 4, 7):
        multiply(slot)

    for copy in samp_copies:
        copy.wait_recv()
    samples = sampsrc[0]
    for r in range(1, GRID):
        samples = samples + sampin[r]
    total_samples[...] = samples
    samples_out = pltpu.make_async_copy(total_samples, samples_ref, load_sem.at[14])
    samples_out.start()
    for copy in results:
        copy.wait_recv()
    for copy in stores:
        copy.wait()
    samples_out.wait()
    field_out.wait()

    sent = halo_copies + list(cell_copies.values()) + samp_copies + list(near_copies.values()) + list(relay_copies.values())
    sent += list(plane_copies.values())
    for copy in sent + [sib_piece, sib_class] + results:
        copy.wait_send()


def merge(
    mine_ref,
    other_ref,
    samples_ref,
    field_ref,
    basis_ref,
    cross_ref,
    out_ref,
    ufinal_ref,
    halves,
    samples,
    bases,
    crossing,
    out,
    field,
    sem,
):
    core = lax.axis_index("sta") % 2
    field_in = pltpu.make_async_copy(field_ref, field, sem.at[0])
    field_out = pltpu.make_async_copy(field, ufinal_ref, sem.at[7])
    loads = [
        pltpu.make_async_copy(samples_ref, samples, sem.at[1]),
        pltpu.make_async_copy(basis_ref, bases, sem.at[2]),
        pltpu.make_async_copy(cross_ref, crossing, sem.at[3]),
    ]
    halves_in = [
        pltpu.make_async_copy(mine_ref, halves.at[core], sem.at[4]),
        pltpu.make_async_copy(other_ref, halves.at[1 - core], sem.at[5]),
    ]
    for copy in loads:
        copy.start()
    for copy in halves_in:
        copy.start()
    field_in.start()
    for copy in loads:
        copy.wait()
    across = jnp.transpose(jnp.concatenate([samples[...], jnp.zeros((120, 128), F32)], axis=0))
    basis = bases[...]
    lowpass = jnp.concatenate([crossing[...], crossing[...]], axis=1)
    weight = lowpass * (1.0 - lowpass)
    low = across[:, 0:1] * basis[0:1, :]
    for step in range(1, STEPS):
        low = low + across[:, step : step + 1] * basis[step : step + 1, :]
    numer = jnp.sum(weight * low * low, axis=1, keepdims=True) * (1.0 / 1024)
    field_in.wait()
    field_out.start()
    for copy in halves_in:
        copy.wait()
    full = jnp.concatenate([halves[0], halves[1]], axis=1)
    denom = jnp.sum(weight * full * full, axis=1, keepdims=True) * (1.0 / 1024)
    ratio = jnp.sqrt((numer + 1e-06) / (denom + 1e-06))
    out[...] = lowpass * low + (1.0 - lowpass) * (ratio * full)
    store = pltpu.make_async_copy(out, out_ref, sem.at[6])
    store.start()
    field_out.wait()
    store.wait()


def local(
    u_now,
    u_prev,
    buoyancy,
    modulus,
    station_cell,
    path_class,
    spectra,
    cos_table,
    sin_table,
    path_filter,
    lf_basis,
    crossover,
):
    dma = pltpu.SemaphoreType.DMA
    anywhere = pl.BlockSpec(memory_space=pl.ANY)
    mine, other, samples, field = pl.pallas_call(
            kernel,
            out_shape=(
                jax.ShapeDtypeStruct((128, 512), F32),
                jax.ShapeDtypeStruct((128, 512), F32),
                jax.ShapeDtypeStruct((8, 128), F32),
                jax.ShapeDtypeStruct((128, 256), F32),
            ),
            in_specs=[anywhere] * 10,
            out_specs=(anywhere,) * 4,
            scratch_shapes=[
                pltpu.VMEM((1, 128), jnp.int32),
                pltpu.VMEM((128, 2048), jnp.int32),
                pltpu.VMEM((128, 512), BF16),
                pltpu.VMEM((128, 512), F32),
                pltpu.VMEM((128, 512), F32),
                pltpu.VMEM((8, 512), F32),
                pltpu.VMEM((128, 256), F32),
                pltpu.VMEM((8, 128), F32),
                pltpu.VMEM((16, 8, 128), jnp.int32),
                pltpu.VMEM((8, 128), jnp.int32),
                pltpu.VMEM((4, 8, 128), F32),
                pltpu.VMEM((2, 4, 8, 256), F32),
                pltpu.VMEM((2, 4, 8, 128), F32),
                pltpu.VMEM((4, 4, 8, 128), F32),
                pltpu.VMEM((4, 136, 384), F32),
                pltpu.VMEM((4, 256, 256), BF16),
                pltpu.VMEM((16, 8, 128), F32),
                pltpu.VMEM((16, 8, 128), F32),
                pltpu.VMEM((128, 2048), BF16),
                pltpu.VMEM((128, 2048), BF16),
                pltpu.VMEM((2, 912, 2048), BF16),
                pltpu.VMEM((2, 2, 64, 512), BF16),
                pltpu.VMEM((8, 2, 2, 64, 512), BF16),
                pltpu.VMEM((2, 128, 512), F32),
                dma((17,)),
                dma((16,)),
                dma((16,)),
                dma((8,)),
                dma((8,)),
                dma((16,)),
                dma((16,)),
                dma((12,)),
                dma((12,)),
                dma((12,)),
                dma((12,)),
                dma((28,)),
                dma((28,)),
                dma((4,)),
                dma((4,)),
            ],
            compiler_params=pltpu.CompilerParams(
                collective_id=0, has_side_effects=True, vmem_limit_bytes=60 * 1024 * 1024
            ),
        )(
            u_now,
            u_prev,
            buoyancy,
            modulus,
            station_cell.reshape(1, 128),
            path_class,
            spectra,
            cos_table,
            sin_table,
            path_filter,
    )
    return pl.pallas_call(
        merge,
        out_shape=(jax.ShapeDtypeStruct((128, 1024), F32), jax.ShapeDtypeStruct((128, 256), F32)),
        in_specs=[anywhere] * 6,
        out_specs=(anywhere,) * 2,
        scratch_shapes=[
            pltpu.VMEM((2, 128, 512), F32),
            pltpu.VMEM((8, 128), F32),
            pltpu.VMEM((4, 1024), F32),
            pltpu.VMEM((1, 512), F32),
            pltpu.VMEM((128, 1024), F32),
            pltpu.VMEM((128, 256), F32),
            dma((8,)),
        ],
        compiler_params=pltpu.CompilerParams(vmem_limit_bytes=60 * 1024 * 1024),
    )(mine, other, samples, field, lf_basis, crossover.reshape(1, 512))


def solution(mesh):
    in_specs = (
        P("grid", "sta"),
        P("grid", "sta"),
        P("grid", "sta"),
        P("grid", "sta"),
        P(("grid", "sta")),
        P(("grid", "sta"), None),
        P("sta", None),
        P("sta", None),
        P("sta", None),
        P(),
        P(),
        P(),
    )
    out_specs = (P(("grid", "sta"), None), P("grid", "sta"))
    return jax.shard_map(local, mesh=mesh, in_specs=in_specs, out_specs=out_specs, check_vma=False)
```

```python
import functools

import jax
import jax.numpy as jnp
from jax import lax
from jax.experimental import pallas as pl
from jax.experimental.pallas import tpu as pltpu
from jax.sharding import PartitionSpec as P

STEPS = 4
CLASSES = 8
MESH = pl.DeviceIdType.MESH
BF16 = jnp.bfloat16
F32 = jnp.float32

SLOTS = ((0, 0), (0, 1), (1, 0), (3, 0), (1, 1), (3, 1), (2, 0), (2, 1))
SIDES = [(0, -1), (0, 1), (-1, -1), (-1, 1), (1, -1), (1, 1)]
HALO = [(-1, 0), (1, 0)] + SIDES
FORWARDED = ((6, 0, 0), (6, 0, 1), (5, 0, 0), (4, 0, 1))
TILT = (0, 0, 2, 1, 0, 2, 0, 0)
GRID = 16
FARTHEST = (8, 9, 7, 10, 6, 11, 5, 12, 4, 13, 3, 14, 2, 15, 1, 0)
SUBCHIP = 256


def kernel(
    u_ref,
    up_ref,
    b_ref,
    m_ref,
    cell_ref,
    class_ref,
    spectra_ref,
    cos_ref,
    sin_ref,
    filter_ref,
    mine_ref,
    other_ref,
    samples_ref,
    field_ref,
    cellraw,
    classraw,
    spectra,
    cosines,
    sines,
    filters,
    final,
    total_samples,
    cells,
    cellsrc,
    colsrc,
    rowin,
    colin,
    cornerin,
    ext,
    ush,
    sampsrc,
    sampin,
    classown,
    classsib,
    onehot,
    phased,
    pieces,
    high,
    load_sem,
    cell_send,
    cell_recv,
    halo_send,
    halo_recv,
    samp_send,
    samp_recv,
    near_send,
    near_recv,
    relay_send,
    relay_recv,
    plane_send,
    plane_recv,
    sib_send,
    sib_recv,
):
    g = lax.axis_index("grid")
    s = lax.axis_index("sta")
    z, xl = g // 2, g % 2
    y, xh, core = s // 4, (s // 2) % 2, s % 2
    colour = (z + xl) % 2

    def along_grid(r):
        return ((g + r) % GRID, s)

    def beside(dg, ds):
        return ((g + dg + 16) % 16, (s + ds + 16) % 16)

    def chip(dy, cross, dc):
        xh2 = (xh + cross) % 2
        xl2 = (xl + cross) % 2
        return (z * 2 + xl2, (((y + dy) % 4) * 2 + xh2) * 2 + (core + dc) % 2)

    sibling = chip(0, 0, 1)
    plane = [((g + 2) % 16, s), ((g + 14) % 16, s), (z * 2 + 1 - xl, s)]
    near = [(dy, cross, dc) for dy, cross in ((1, 0), (3, 0), (0, 1)) for dc in (0, 1)]
    partners = [chip(*o) for o in near] + [sibling]
    partners += [beside(*o) for o in SIDES]
    partners += [along_grid(r) for r in range(1, GRID)]
    barrier = pltpu.get_barrier_semaphore()
    for partner in partners:
        pl.semaphore_signal(barrier, inc=1, device_id=partner, device_id_type=MESH)

    def load(i, src, dst):
        copy = pltpu.make_async_copy(src, dst, load_sem.at[i])
        copy.start()
        return copy

    load_cell = load(0, cell_ref, cellraw)
    load_phase = [load(5, spectra_ref, spectra), load(6, cos_ref, cosines), load(7, sin_ref, sines)]
    load_grid = [
        load(1 + a, ref, ext.at[a, pl.ds(0, 128), pl.ds(0, 256)])
        for a, ref in enumerate((u_ref, up_ref, b_ref, m_ref))
    ]
    load_class = load(8, class_ref, classraw)
    load_filter = load(9, filter_ref, filters)

    load_cell.wait()
    cellsrc[...] = jnp.broadcast_to(cellraw[...], (8, 128))
    for copy in load_phase:
        copy.wait()
    wide = spectra[...].astype(F32)
    phased[0] = (wide * cosines[...]).astype(BF16).reshape(2, 64, 512)
    phased[1] = (wide * sines[...]).astype(BF16).reshape(2, 64, 512)
    lane = lax.broadcasted_iota(jnp.int32, (128, 128), 1)
    packed = jnp.zeros((128, 128), F32)
    for a in range(4):
        load_grid[a].wait()
        both = jnp.where(lane < 64, ext[a, 0:128, 0:128], ext[a, 0:128, 128:256])
        packed = jnp.where(lane // 8 == a, pltpu.roll(both, 8 * a + 4, 1), packed)
    colsrc[...] = jnp.transpose(packed)[0:32].reshape(4, 8, 128)

    def expand(which, classes):
        held = classes[...]
        for c in range(1, CLASSES):
            onehot[which, (c - 1) * 128 : c * 128, :] = jnp.where(held == BF16(c), BF16(1), BF16(0))
        onehot[which, 896:912, :] = jnp.ones((16, 2048), BF16)


    pl.semaphore_wait(barrier, len(partners))

    def remote(src, dst, send, recv, target):
        copy = pltpu.make_async_remote_copy(
            src_ref=src, dst_ref=dst, send_sem=send, recv_sem=recv, device_id=target, device_id_type=MESH
        )
        copy.start()
        return copy

    halo_copies = []
    for i, (dg, ds) in enumerate(HALO):
        side = 1 if dg == 1 else 0
        rows = pl.ds(120 * side, 8)
        if ds == 0:
            src, dst = ext.at[:, rows, pl.ds(0, 256)], rowin.at[side]
        elif dg == 0:
            src, dst = colsrc, colin.at[1 if ds == 1 else 0]
        else:
            half = 1 if ds == 1 else 0
            src, dst = ext.at[:, rows, pl.ds(half * 128, 128)], cornerin.at[side * 2 + half]
        halo_copies.append(remote(src, dst, halo_send.at[i], halo_recv.at[i], beside(dg, ds)))
    cell_copies = {
        GRID - r: remote(cellsrc, cells.at[GRID - r], cell_send.at[r], cell_recv.at[r], along_grid(r))
        for r in FARTHEST
        if r
    }
    near_copies = {}

    def send_near(turn):
        for i, (dy, cross, dc) in enumerate(near):
            slot = SLOTS.index(((4 - dy) % 4, cross))
            half = 1 - colour if cross else colour
            part = 1 - turn if dy == 3 else turn
            rows = pl.ds(32 * part, 32)
            near_copies[dy, cross, dc, part] = remote(
                phased.at[(core + dc) % 2, half, rows],
                pieces.at[slot, core, half, rows],
                near_send.at[2 * i + part],
                near_recv.at[2 * i + part],
                chip(dy, cross, dc),
            )

    send_near(0)
    sib_piece = remote(phased.at[1 - core], pieces.at[0, core], sib_send.at[0], sib_recv.at[0], sibling)

    relay_copies = {}

    def relay(source, dy, cross, slot, part):
        i = len(relay_copies)
        rows = pl.ds(32 * part, 32)
        relay_copies[slot, cross, part] = remote(
            pieces.at[source, :, colour, rows],
            pieces.at[slot, :, colour, rows],
            relay_send.at[i],
            relay_recv.at[i],
            chip(dy, cross, 0),
        )

    plane_copies = {}

    def share(slot, part, half):
        for quarter in (2 * part, 2 * part + 1):
            rows = pieces.at[slot, :, half, pl.ds(16 * quarter, 16)]
            i = (slot - 1) * 4 + quarter
            plane_copies[slot, quarter] = remote(rows, rows, plane_send.at[i], plane_recv.at[i], plane[(i + TILT[slot]) % 3])

    load_class.wait()
    for slot, (dy, cross) in enumerate(SLOTS):
        source = ((y + dy) % 4) * 2 + (xh + cross) % 2
        columns = pl.ds(pl.multiple_of(source * SUBCHIP, SUBCHIP), SUBCHIP)
        classown[:, slot * SUBCHIP : (slot + 1) * SUBCHIP] = classraw[:, columns].astype(F32).astype(BF16)
    sib_class = remote(classown, classsib, sib_send.at[1], sib_recv.at[1], sibling)
    expand(0, classown)
    pieces[0, core] = phased[core]
    cells[0] = cellsrc[...]

    sib_piece.wait_recv()
    send_near(1)
    sib_class.wait_recv()
    expand(1, classsib)
    load_filter.wait()

    results, stores = [], []

    def multiply(slot):
        for quarter in range(4):
            if (slot, quarter) in plane_copies:
                plane_copies[slot, quarter].wait_recv()
        for cross, part in ((0, 0), (0, 1), (1, 0), (1, 1)):
            if (slot, cross, part) in relay_copies and (slot, cross, part) not in FORWARDED:
                relay_copies[slot, cross, part].wait_recv()
        part = pl.ds(slot * SUBCHIP, SUBCHIP)
        for n in (0, 256):
            weights = pieces[slot, :, :, :, n : n + 256].reshape(SUBCHIP, 256)
            first = filters[0:1, n : n + 256]
            total = jnp.dot(onehot[0, 896:912, part], weights, preferred_element_type=F32)
            acc = first * total[0:1]
            for c in range(1, CLASSES):
                lhs = onehot[:, (c - 1) * 128 : c * 128, part].reshape(256, SUBCHIP)
                acc = acc + (filters[c : c + 1, n : n + 256] - first) * jnp.dot(
                    lhs, weights, preferred_element_type=F32
                )
            acc = acc.reshape(2, 128, 256)
            if slot == 0:
                high[:, :, n : n + 256] = acc
            else:
                high[:, :, n : n + 256] += acc
            if slot == 7:
                done = pl.ds(n, 256)
                i = 2 + n // 256
                results.append(
                    remote(high.at[1, :, done], other_ref.at[:, done], sib_send.at[i], sib_recv.at[i], sibling)
                )
                mine_out = pltpu.make_async_copy(high.at[0, :, done], mine_ref.at[:, done], load_sem.at[13 + i])
                mine_out.start()
                stores.append(mine_out)

    multiply(0)

    def arrived(dy, cross, part):
        for dc in (0, 1):
            near_copies[dy, cross, dc, part].wait_recv()

    for copy in ((1, 0, 0), (3, 0, 1), (0, 1, 0)):
        arrived(*copy)
    relay(3, 1, 0, 6, 0)
    relay(2, 3, 0, 6, 1)
    share(3, 0, colour)
    share(2, 1, colour)
    share(1, 0, colour)

    for copy in halo_copies:
        copy.wait_recv()
    zero = F32(0)
    lane8 = lax.broadcasted_iota(jnp.int32, (8, 128), 1)
    sub8 = lax.broadcasted_iota(jnp.int32, (8, 128), 0)
    sub8w = lax.broadcasted_iota(jnp.int32, (8, 256), 0)
    below, above = g < 15, g > 0
    right, left = s < 15, s > 0
    sides = []
    for a in range(4):
        sides.append(
            jnp.where(sub8 < 4, jnp.where(left, colin[1, a], zero), jnp.where(right, colin[0, a], zero))
        )
    columns = jnp.transpose(jnp.concatenate(sides + [jnp.zeros((96, 128), F32)], axis=0))
    for a in range(4):
        ext[a, 0:128, 256:384] = pltpu.roll(columns, 128 - (8 * a + 4), 1)
        ext[a, 128:136, 0:256] = jnp.where(
            sub8w < 4, jnp.where(below, rowin[0, a], zero), jnp.where(above, rowin[1, a], zero)
        )
        ext[a, 128:136, 256:384] = jnp.where(
            sub8 < 4,
            jnp.where(
                lane8 < 64,
                jnp.where(below & right, cornerin[0, a], zero),
                jnp.where(below & left, cornerin[1, a], zero),
            ),
            jnp.where(
                lane8 < 64,
                jnp.where(above & right, cornerin[2, a], zero),
                jnp.where(above & left, cornerin[3, a], zero),
            ),
        )
    current, previous, buoyancy, modulus = ext[0], ext[1], ext[2], ext[3]
    rows, cols = current.shape
    down = 0.5 * (modulus + pltpu.roll(modulus, rows - 1, 0))
    along = 0.5 * (modulus + pltpu.roll(modulus, cols - 1, 1))
    for step in range(STEPS):
        flux_x = down * (pltpu.roll(current, rows - 1, 0) - current)
        flux_y = along * (pltpu.roll(current, cols - 1, 1) - current)
        div = flux_x - pltpu.roll(flux_x, 1, 0) + flux_y - pltpu.roll(flux_y, 1, 1)
        following = 2.0 * current - previous + buoyancy * div
        previous, current = current, following
        block = current[0:128, 0:256]
        coarse = block.astype(BF16)
        ush[step, 0:128, :] = coarse
        ush[step, 128:256, :] = (block - coarse.astype(F32)).astype(BF16)
        if step == STEPS - 1:
            final[...] = block

    field_out = pltpu.make_async_copy(final, field_ref, load_sem.at[13])
    field_out.start()

    for copy in ((1, 0, 1), (3, 0, 0), (0, 1, 1)):
        arrived(*copy)
    relay(1, 1, 0, 5, 0)
    relay(1, 3, 0, 4, 1)
    relay(3, 0, 1, 5, 1)
    relay(2, 0, 1, 4, 0)
    share(1, 1, colour)
    share(3, 1, colour)
    share(2, 0, colour)

    row_at = lax.broadcasted_iota(jnp.int32, (128, 128), 0)
    col_at = lax.broadcasted_iota(jnp.int32, (256, 128), 0)
    samp_copies = []
    for pair in range(0, GRID, 2):
        pair = FARTHEST[14 - pair : 16 - pair]
        for r in pair:
            if r > 0:
                cell_copies[r].wait_recv()
        picks, inside = [], []
        for r in pair:
            cell = cells[r, 0:1, :]
            row = lax.shift_right_logical(cell, 12) - g * 128
            col = lax.bitwise_and(cell, 4095) - s * 256
            picks.append(jnp.where(col_at == col, F32(1), zero).astype(BF16))
            inside.append(row_at == row)
        found = jnp.dot(
            ush[...].reshape(4 * 256, 256), jnp.concatenate(picks, axis=1), preferred_element_type=F32
        )
        mask = jnp.concatenate(inside, axis=1)
        recorded = []
        for step in range(STEPS):
            both = found[step * 256 : step * 256 + 128] + found[step * 256 + 128 : step * 256 + 256]
            recorded.append(jnp.sum(jnp.where(mask, both, zero), axis=0, keepdims=True))
        recorded = jnp.concatenate(recorded + [jnp.zeros((4, 256), F32)], axis=0)
        sampsrc[pair[0]] = recorded[:, 0:128]
        sampsrc[pair[1]] = recorded[:, 128:256]
        for r in pair:
            if r > 0:
                samp_copies.append(
                    remote(sampsrc.at[r], sampin.at[GRID - r], samp_send.at[r], samp_recv.at[r], along_grid(r))
                )

    relay(1, 1, 0, 5, 1)
    relay(1, 3, 0, 4, 0)
    relay_copies[6, 0, 0].wait_recv()
    relay_copies[6, 0, 1].wait_recv()
    relay(6, 0, 1, 7, 0)
    relay(6, 0, 1, 7, 1)
    share(6, 0, colour)
    share(6, 1, colour)
    relay_copies[5, 0, 0].wait_recv()
    relay(5, 1, 0, 7, 0)
    relay_copies[4, 0, 1].wait_recv()
    relay(4, 3, 0, 7, 1)
    share(5, 0, colour)
    share(4, 1, colour)
    for slot in (1, 2, 3, 6, 5, 4, 7):
        multiply(slot)

    for copy in samp_copies:
        copy.wait_recv()
    samples = sampsrc[0]
    for r in range(1, GRID):
        samples = samples + sampin[r]
    total_samples[...] = samples
    samples_out = pltpu.make_async_copy(total_samples, samples_ref, load_sem.at[14])
    samples_out.start()
    for copy in results:
        copy.wait_recv()
    for copy in stores:
        copy.wait()
    samples_out.wait()
    field_out.wait()

    sent = halo_copies + list(cell_copies.values()) + samp_copies + list(near_copies.values()) + list(relay_copies.values())
    sent += list(plane_copies.values())
    for copy in sent + [sib_piece, sib_class] + results:
        copy.wait_send()


def merge(
    mine_ref,
    other_ref,
    samples_ref,
    field_ref,
    basis_ref,
    cross_ref,
    out_ref,
    ufinal_ref,
    halves,
    samples,
    bases,
    crossing,
    out,
    field,
    sem,
):
    core = lax.axis_index("sta") % 2
    field_in = pltpu.make_async_copy(field_ref, field, sem.at[0])
    field_out = pltpu.make_async_copy(field, ufinal_ref, sem.at[7])
    loads = [
        pltpu.make_async_copy(samples_ref, samples, sem.at[1]),
        pltpu.make_async_copy(basis_ref, bases, sem.at[2]),
        pltpu.make_async_copy(cross_ref, crossing, sem.at[3]),
    ]
    halves_in = [
        pltpu.make_async_copy(mine_ref, halves.at[core], sem.at[4]),
        pltpu.make_async_copy(other_ref, halves.at[1 - core], sem.at[5]),
    ]
    for copy in loads:
        copy.start()
    for copy in halves_in:
        copy.start()
    field_in.start()
    for copy in loads:
        copy.wait()
    across = jnp.transpose(jnp.concatenate([samples[...], jnp.zeros((120, 128), F32)], axis=0))
    basis = bases[...]
    lowpass = jnp.concatenate([crossing[...], crossing[...]], axis=1)
    weight = lowpass * (1.0 - lowpass)
    low = across[:, 0:1] * basis[0:1, :]
    for step in range(1, STEPS):
        low = low + across[:, step : step + 1] * basis[step : step + 1, :]
    numer = jnp.sum(weight * low * low, axis=1, keepdims=True) * (1.0 / 1024)
    field_in.wait()
    field_out.start()
    for copy in halves_in:
        copy.wait()
    full = jnp.concatenate([halves[0], halves[1]], axis=1)
    denom = jnp.sum(weight * full * full, axis=1, keepdims=True) * (1.0 / 1024)
    ratio = jnp.sqrt((numer + 1e-06) / (denom + 1e-06))
    out[...] = lowpass * low + (1.0 - lowpass) * (ratio * full)
    store = pltpu.make_async_copy(out, out_ref, sem.at[6])
    store.start()
    field_out.wait()
    store.wait()


def local(
    u_now,
    u_prev,
    buoyancy,
    modulus,
    station_cell,
    path_class,
    spectra,
    cos_table,
    sin_table,
    path_filter,
    lf_basis,
    crossover,
):
    dma = pltpu.SemaphoreType.DMA
    anywhere = pl.BlockSpec(memory_space=pl.ANY)
    mine, other, samples, field = pl.pallas_call(
            kernel,
            out_shape=(
                jax.ShapeDtypeStruct((128, 512), F32),
                jax.ShapeDtypeStruct((128, 512), F32),
                jax.ShapeDtypeStruct((8, 128), F32),
                jax.ShapeDtypeStruct((128, 256), F32),
            ),
            in_specs=[anywhere] * 10,
            out_specs=(anywhere,) * 4,
            scratch_shapes=[
                pltpu.VMEM((1, 128), jnp.int32),
                pltpu.VMEM((128, 2048), jnp.int32),
                pltpu.VMEM((128, 512), BF16),
                pltpu.VMEM((128, 512), F32),
                pltpu.VMEM((128, 512), F32),
                pltpu.VMEM((8, 512), F32),
                pltpu.VMEM((128, 256), F32),
                pltpu.VMEM((8, 128), F32),
                pltpu.VMEM((16, 8, 128), jnp.int32),
                pltpu.VMEM((8, 128), jnp.int32),
                pltpu.VMEM((4, 8, 128), F32),
                pltpu.VMEM((2, 4, 8, 256), F32),
                pltpu.VMEM((2, 4, 8, 128), F32),
                pltpu.VMEM((4, 4, 8, 128), F32),
                pltpu.VMEM((4, 136, 384), F32),
                pltpu.VMEM((4, 256, 256), BF16),
                pltpu.VMEM((16, 8, 128), F32),
                pltpu.VMEM((16, 8, 128), F32),
                pltpu.VMEM((128, 2048), BF16),
                pltpu.VMEM((128, 2048), BF16),
                pltpu.VMEM((2, 912, 2048), BF16),
                pltpu.VMEM((2, 2, 64, 512), BF16),
                pltpu.VMEM((8, 2, 2, 64, 512), BF16),
                pltpu.VMEM((2, 128, 512), F32),
                dma((17,)),
                dma((16,)),
                dma((16,)),
                dma((8,)),
                dma((8,)),
                dma((16,)),
                dma((16,)),
                dma((12,)),
                dma((12,)),
                dma((12,)),
                dma((12,)),
                dma((28,)),
                dma((28,)),
                dma((4,)),
                dma((4,)),
            ],
            compiler_params=pltpu.CompilerParams(
                collective_id=0, has_side_effects=True, vmem_limit_bytes=60 * 1024 * 1024
            ),
        )(
            u_now,
            u_prev,
            buoyancy,
            modulus,
            station_cell.reshape(1, 128),
            path_class,
            spectra,
            cos_table,
            sin_table,
            path_filter,
    )
    return pl.pallas_call(
        merge,
        out_shape=(jax.ShapeDtypeStruct((128, 1024), F32), jax.ShapeDtypeStruct((128, 256), F32)),
        in_specs=[anywhere] * 6,
        out_specs=(anywhere,) * 2,
        scratch_shapes=[
            pltpu.VMEM((2, 128, 512), F32),
            pltpu.VMEM((8, 128), F32),
            pltpu.VMEM((4, 1024), F32),
            pltpu.VMEM((1, 512), F32),
            pltpu.VMEM((128, 1024), F32),
            pltpu.VMEM((128, 256), F32),
            dma((8,)),
        ],
        compiler_params=pltpu.CompilerParams(vmem_limit_bytes=60 * 1024 * 1024),
    )(mine, other, samples, field, lf_basis, crossover.reshape(1, 512))


def solution(mesh):
    in_specs = (
        P("grid", "sta"),
        P("grid", "sta"),
        P("grid", "sta"),
        P("grid", "sta"),
        P(("grid", "sta")),
        P(("grid", "sta"), None),
        P("sta", None),
        P("sta", None),
        P("sta", None),
        P(),
        P(),
        P(),
    )
    out_specs = (P(("grid", "sta"), None), P("grid", "sta"))
    return jax.shard_map(local, mesh=mesh, in_specs=in_specs, out_specs=out_specs, check_vma=False)
```

```python
import functools

import jax
import jax.numpy as jnp
from jax import lax
from jax.experimental import pallas as pl
from jax.experimental.pallas import tpu as pltpu
from jax.sharding import PartitionSpec as P

STEPS = 4
CLASSES = 8
MESH = pl.DeviceIdType.MESH
BF16 = jnp.bfloat16
F32 = jnp.float32

SLOTS = ((0, 0), (0, 1), (1, 0), (3, 0), (1, 1), (3, 1), (2, 0), (2, 1))
SIDES = [(0, -1), (0, 1), (-1, -1), (-1, 1), (1, -1), (1, 1)]
HALO = [(-1, 0), (1, 0)] + SIDES
FORWARDED = ((6, 0, 0), (6, 0, 1), (5, 0, 0), (4, 0, 1))
TILT = (0, 0, 2, 1, 0, 2, 0, 0)
GRID = 16
FARTHEST = (8, 9, 7, 10, 6, 11, 5, 12, 4, 13, 3, 14, 2, 15, 1, 0)
SUBCHIP = 256


def kernel(
    u_ref,
    up_ref,
    b_ref,
    m_ref,
    cell_ref,
    class_ref,
    spectra_ref,
    cos_ref,
    sin_ref,
    filter_ref,
    mine_ref,
    other_ref,
    samples_ref,
    field_ref,
    cellraw,
    classraw,
    spectra,
    cosines,
    sines,
    filters,
    final,
    total_samples,
    cells,
    cellsrc,
    colsrc,
    rowin,
    colin,
    cornerin,
    ext,
    ush,
    sampsrc,
    sampin,
    classown,
    classsib,
    onehot,
    phased,
    pieces,
    high,
    load_sem,
    cell_send,
    cell_recv,
    halo_send,
    halo_recv,
    samp_send,
    samp_recv,
    near_send,
    near_recv,
    relay_send,
    relay_recv,
    plane_send,
    plane_recv,
    sib_send,
    sib_recv,
):
    g = lax.axis_index("grid")
    s = lax.axis_index("sta")
    z, xl = g // 2, g % 2
    y, xh, core = s // 4, (s // 2) % 2, s % 2
    colour = (z + xl) % 2

    def along_grid(r):
        return ((g + r) % GRID, s)

    def beside(dg, ds):
        return ((g + dg + 16) % 16, (s + ds + 16) % 16)

    def chip(dy, cross, dc):
        xh2 = (xh + cross) % 2
        xl2 = (xl + cross) % 2
        return (z * 2 + xl2, (((y + dy) % 4) * 2 + xh2) * 2 + (core + dc) % 2)

    sibling = chip(0, 0, 1)
    plane = [((g + 2) % 16, s), ((g + 14) % 16, s), (z * 2 + 1 - xl, s)]
    near = [(dy, cross, dc) for dy, cross in ((1, 0), (3, 0), (0, 1)) for dc in (0, 1)]
    partners = [chip(*o) for o in near] + [sibling]
    partners += [beside(*o) for o in SIDES]
    partners += [along_grid(r) for r in range(1, GRID)]
    barrier = pltpu.get_barrier_semaphore()
    for partner in partners:
        pl.semaphore_signal(barrier, inc=1, device_id=partner, device_id_type=MESH)

    def load(i, src, dst):
        copy = pltpu.make_async_copy(src, dst, load_sem.at[i])
        copy.start()
        return copy

    load_cell = load(0, cell_ref, cellraw)
    load_phase = [load(5, spectra_ref, spectra), load(6, cos_ref, cosines), load(7, sin_ref, sines)]
    load_grid = [
        load(1 + a, ref, ext.at[a, pl.ds(0, 128), pl.ds(0, 256)])
        for a, ref in enumerate((u_ref, up_ref, b_ref, m_ref))
    ]
    load_class = load(8, class_ref, classraw)
    load_filter = load(9, filter_ref, filters)

    load_cell.wait()
    cellsrc[...] = jnp.broadcast_to(cellraw[...], (8, 128))
    for copy in load_phase:
        copy.wait()
    wide = spectra[...].astype(F32)
    phased[0] = (wide * cosines[...]).astype(BF16).reshape(2, 64, 512)
    phased[1] = (wide * sines[...]).astype(BF16).reshape(2, 64, 512)
    lane = lax.broadcasted_iota(jnp.int32, (128, 128), 1)
    packed = jnp.zeros((128, 128), F32)
    for a in range(4):
        load_grid[a].wait()
        both = jnp.where(lane < 64, ext[a, 0:128, 0:128], ext[a, 0:128, 128:256])
        packed = jnp.where(lane // 8 == a, pltpu.roll(both, 8 * a + 4, 1), packed)
    colsrc[...] = jnp.transpose(packed)[0:32].reshape(4, 8, 128)

    def expand(which, classes):
        held = classes[...]
        for c in range(1, CLASSES):
            onehot[which, (c - 1) * 128 : c * 128, :] = jnp.where(held == BF16(c), BF16(1), BF16(0))
        onehot[which, 896:912, :] = jnp.ones((16, 2048), BF16)


    pl.semaphore_wait(barrier, len(partners))

    def remote(src, dst, send, recv, target):
        copy = pltpu.make_async_remote_copy(
            src_ref=src, dst_ref=dst, send_sem=send, recv_sem=recv, device_id=target, device_id_type=MESH
        )
        copy.start()
        return copy

    halo_copies = []
    for i, (dg, ds) in enumerate(HALO):
        side = 1 if dg == 1 else 0
        rows = pl.ds(120 * side, 8)
        if ds == 0:
            src, dst = ext.at[:, rows, pl.ds(0, 256)], rowin.at[side]
        elif dg == 0:
            src, dst = colsrc, colin.at[1 if ds == 1 else 0]
        else:
            half = 1 if ds == 1 else 0
            src, dst = ext.at[:, rows, pl.ds(half * 128, 128)], cornerin.at[side * 2 + half]
        halo_copies.append(remote(src, dst, halo_send.at[i], halo_recv.at[i], beside(dg, ds)))
    cell_copies = {
        GRID - r: remote(cellsrc, cells.at[GRID - r], cell_send.at[r], cell_recv.at[r], along_grid(r))
        for r in FARTHEST
        if r
    }
    near_copies = {}

    def send_near(turn):
        for i, (dy, cross, dc) in enumerate(near):
            slot = SLOTS.index(((4 - dy) % 4, cross))
            half = 1 - colour if cross else colour
            part = 1 - turn if dy == 3 else turn
            rows = pl.ds(32 * part, 32)
            near_copies[dy, cross, dc, part] = remote(
                phased.at[(core + dc) % 2, half, rows],
                pieces.at[slot, core, half, rows],
                near_send.at[2 * i + part],
                near_recv.at[2 * i + part],
                chip(dy, cross, dc),
            )

    send_near(0)
    sib_piece = remote(phased.at[1 - core], pieces.at[0, core], sib_send.at[0], sib_recv.at[0], sibling)

    relay_copies = {}

    def relay(source, dy, cross, slot, part):
        i = len(relay_copies)
        rows = pl.ds(32 * part, 32)
        relay_copies[slot, cross, part] = remote(
            pieces.at[source, :, colour, rows],
            pieces.at[slot, :, colour, rows],
            relay_send.at[i],
            relay_recv.at[i],
            chip(dy, cross, 0),
        )

    plane_copies = {}

    def share(slot, part, half):
        for quarter in (2 * part, 2 * part + 1):
            rows = pieces.at[slot, :, half, pl.ds(16 * quarter, 16)]
            i = (slot - 1) * 4 + quarter
            plane_copies[slot, quarter] = remote(rows, rows, plane_send.at[i], plane_recv.at[i], plane[(i + TILT[slot]) % 3])

    load_class.wait()
    for slot, (dy, cross) in enumerate(SLOTS):
        source = ((y + dy) % 4) * 2 + (xh + cross) % 2
        columns = pl.ds(pl.multiple_of(source * SUBCHIP, SUBCHIP), SUBCHIP)
        classown[:, slot * SUBCHIP : (slot + 1) * SUBCHIP] = classraw[:, columns].astype(F32).astype(BF16)
    sib_class = remote(classown, classsib, sib_send.at[1], sib_recv.at[1], sibling)
    expand(0, classown)
    pieces[0, core] = phased[core]
    cells[0] = cellsrc[...]

    sib_piece.wait_recv()
    send_near(1)
    sib_class.wait_recv()
    expand(1, classsib)
    load_filter.wait()

    results, stores = [], []

    def multiply(slot):
        for quarter in range(4):
            if (slot, quarter) in plane_copies:
                plane_copies[slot, quarter].wait_recv()
        for cross, part in ((0, 0), (0, 1), (1, 0), (1, 1)):
            if (slot, cross, part) in relay_copies and (slot, cross, part) not in FORWARDED:
                relay_copies[slot, cross, part].wait_recv()
        part = pl.ds(slot * SUBCHIP, SUBCHIP)
        for n in (0, 256):
            weights = pieces[slot, :, :, :, n : n + 256].reshape(SUBCHIP, 256)
            first = filters[0:1, n : n + 256]
            total = jnp.dot(onehot[0, 896:912, part], weights, preferred_element_type=F32)
            acc = first * total[0:1]
            for c in range(1, CLASSES):
                lhs = onehot[:, (c - 1) * 128 : c * 128, part].reshape(256, SUBCHIP)
                acc = acc + (filters[c : c + 1, n : n + 256] - first) * jnp.dot(
                    lhs, weights, preferred_element_type=F32
                )
            acc = acc.reshape(2, 128, 256)
            if slot == 0:
                high[:, :, n : n + 256] = acc
            else:
                high[:, :, n : n + 256] += acc
            if slot == 7:
                done = pl.ds(n, 256)
                i = 2 + n // 256
                results.append(
                    remote(high.at[1, :, done], other_ref.at[:, done], sib_send.at[i], sib_recv.at[i], sibling)
                )
                mine_out = pltpu.make_async_copy(high.at[0, :, done], mine_ref.at[:, done], load_sem.at[13 + i])
                mine_out.start()
                stores.append(mine_out)

    multiply(0)

    def arrived(dy, cross, part):
        for dc in (0, 1):
            near_copies[dy, cross, dc, part].wait_recv()

    for copy in ((1, 0, 0), (3, 0, 1), (0, 1, 0)):
        arrived(*copy)
    relay(3, 1, 0, 6, 0)
    relay(2, 3, 0, 6, 1)
    share(3, 0, colour)
    share(2, 1, colour)
    share(1, 0, colour)

    for copy in halo_copies:
        copy.wait_recv()
    zero = F32(0)
    lane8 = lax.broadcasted_iota(jnp.int32, (8, 128), 1)
    sub8 = lax.broadcasted_iota(jnp.int32, (8, 128), 0)
    sub8w = lax.broadcasted_iota(jnp.int32, (8, 256), 0)
    below, above = g < 15, g > 0
    right, left = s < 15, s > 0
    sides = []
    for a in range(4):
        sides.append(
            jnp.where(sub8 < 4, jnp.where(left, colin[1, a], zero), jnp.where(right, colin[0, a], zero))
        )
    columns = jnp.transpose(jnp.concatenate(sides + [jnp.zeros((96, 128), F32)], axis=0))
    for a in range(4):
        ext[a, 0:128, 256:384] = pltpu.roll(columns, 128 - (8 * a + 4), 1)
        ext[a, 128:136, 0:256] = jnp.where(
            sub8w < 4, jnp.where(below, rowin[0, a], zero), jnp.where(above, rowin[1, a], zero)
        )
        ext[a, 128:136, 256:384] = jnp.where(
            sub8 < 4,
            jnp.where(
                lane8 < 64,
                jnp.where(below & right, cornerin[0, a], zero),
                jnp.where(below & left, cornerin[1, a], zero),
            ),
            jnp.where(
                lane8 < 64,
                jnp.where(above & right, cornerin[2, a], zero),
                jnp.where(above & left, cornerin[3, a], zero),
            ),
        )
    current, previous, buoyancy, modulus = ext[0], ext[1], ext[2], ext[3]
    rows, cols = current.shape
    down = 0.5 * (modulus + pltpu.roll(modulus, rows - 1, 0))
    along = 0.5 * (modulus + pltpu.roll(modulus, cols - 1, 1))
    for step in range(STEPS):
        flux_x = down * (pltpu.roll(current, rows - 1, 0) - current)
        flux_y = along * (pltpu.roll(current, cols - 1, 1) - current)
        div = flux_x - pltpu.roll(flux_x, 1, 0) + flux_y - pltpu.roll(flux_y, 1, 1)
        following = 2.0 * current - previous + buoyancy * div
        previous, current = current, following
        block = current[0:128, 0:256]
        coarse = block.astype(BF16)
        ush[step, 0:128, :] = coarse
        ush[step, 128:256, :] = (block - coarse.astype(F32)).astype(BF16)
        if step == STEPS - 1:
            final[...] = block

    field_out = pltpu.make_async_copy(final, field_ref, load_sem.at[13])
    field_out.start()

    for copy in ((1, 0, 1), (3, 0, 0), (0, 1, 1)):
        arrived(*copy)
    relay(1, 1, 0, 5, 0)
    relay(1, 3, 0, 4, 1)
    relay(3, 0, 1, 5, 1)
    relay(2, 0, 1, 4, 0)
    share(1, 1, colour)
    share(3, 1, colour)
    share(2, 0, colour)

    row_at = lax.broadcasted_iota(jnp.int32, (128, 128), 0)
    col_at = lax.broadcasted_iota(jnp.int32, (256, 128), 0)
    samp_copies = []

    def look_up(first, last):
        for pair in range(first, last, 2):
            pair = FARTHEST[pair : pair + 2]
            for r in pair:
                if r > 0:
                    cell_copies[r].wait_recv()
            picks, inside = [], []
            for r in pair:
                cell = cells[r, 0:1, :]
                row = lax.shift_right_logical(cell, 12) - g * 128
                col = lax.bitwise_and(cell, 4095) - s * 256
                picks.append(jnp.where(col_at == col, F32(1), zero).astype(BF16))
                inside.append(row_at == row)
            found = jnp.dot(
                ush[...].reshape(4 * 256, 256), jnp.concatenate(picks, axis=1), preferred_element_type=F32
            )
            mask = jnp.concatenate(inside, axis=1)
            recorded = []
            for step in range(STEPS):
                both = found[step * 256 : step * 256 + 128] + found[step * 256 + 128 : step * 256 + 256]
                recorded.append(jnp.sum(jnp.where(mask, both, zero), axis=0, keepdims=True))
            recorded = jnp.concatenate(recorded + [jnp.zeros((4, 256), F32)], axis=0)
            sampsrc[pair[0]] = recorded[:, 0:128]
            sampsrc[pair[1]] = recorded[:, 128:256]
            for r in pair:
                if r > 0:
                    samp_copies.append(
                        remote(sampsrc.at[r], sampin.at[GRID - r], samp_send.at[r], samp_recv.at[r], along_grid(r))
                    )

    look_up(0, GRID // 2)

    relay(1, 1, 0, 5, 1)
    relay(1, 3, 0, 4, 0)
    relay_copies[6, 0, 0].wait_recv()
    relay_copies[6, 0, 1].wait_recv()
    relay(6, 0, 1, 7, 0)
    relay(6, 0, 1, 7, 1)
    share(6, 0, colour)
    share(6, 1, colour)
    look_up(GRID // 2, GRID)
    relay_copies[5, 0, 0].wait_recv()
    relay(5, 1, 0, 7, 0)
    relay_copies[4, 0, 1].wait_recv()
    relay(4, 3, 0, 7, 1)
    share(5, 0, colour)
    share(4, 1, colour)
    for slot in (1, 2, 3, 6, 5, 4, 7):
        multiply(slot)

    for copy in samp_copies:
        copy.wait_recv()
    samples = sampsrc[0]
    for r in range(1, GRID):
        samples = samples + sampin[r]
    total_samples[...] = samples
    samples_out = pltpu.make_async_copy(total_samples, samples_ref, load_sem.at[14])
    samples_out.start()
    for copy in results:
        copy.wait_recv()
    for copy in stores:
        copy.wait()
    samples_out.wait()
    field_out.wait()

    sent = halo_copies + list(cell_copies.values()) + samp_copies + list(near_copies.values()) + list(relay_copies.values())
    sent += list(plane_copies.values())
    for copy in sent + [sib_piece, sib_class] + results:
        copy.wait_send()


def merge(
    mine_ref,
    other_ref,
    samples_ref,
    field_ref,
    basis_ref,
    cross_ref,
    out_ref,
    ufinal_ref,
    halves,
    samples,
    bases,
    crossing,
    out,
    field,
    sem,
):
    core = lax.axis_index("sta") % 2
    field_in = pltpu.make_async_copy(field_ref, field, sem.at[0])
    field_out = pltpu.make_async_copy(field, ufinal_ref, sem.at[7])
    loads = [
        pltpu.make_async_copy(samples_ref, samples, sem.at[1]),
        pltpu.make_async_copy(basis_ref, bases, sem.at[2]),
        pltpu.make_async_copy(cross_ref, crossing, sem.at[3]),
    ]
    halves_in = [
        pltpu.make_async_copy(mine_ref, halves.at[core], sem.at[4]),
        pltpu.make_async_copy(other_ref, halves.at[1 - core], sem.at[5]),
    ]
    for copy in loads:
        copy.start()
    for copy in halves_in:
        copy.start()
    field_in.start()
    for copy in loads:
        copy.wait()
    across = jnp.transpose(jnp.concatenate([samples[...], jnp.zeros((120, 128), F32)], axis=0))
    basis = bases[...]
    lowpass = jnp.concatenate([crossing[...], crossing[...]], axis=1)
    weight = lowpass * (1.0 - lowpass)
    low = across[:, 0:1] * basis[0:1, :]
    for step in range(1, STEPS):
        low = low + across[:, step : step + 1] * basis[step : step + 1, :]
    numer = jnp.sum(weight * low * low, axis=1, keepdims=True) * (1.0 / 1024)
    field_in.wait()
    field_out.start()
    for copy in halves_in:
        copy.wait()
    full = jnp.concatenate([halves[0], halves[1]], axis=1)
    denom = jnp.sum(weight * full * full, axis=1, keepdims=True) * (1.0 / 1024)
    ratio = jnp.sqrt((numer + 1e-06) / (denom + 1e-06))
    out[...] = lowpass * low + (1.0 - lowpass) * (ratio * full)
    store = pltpu.make_async_copy(out, out_ref, sem.at[6])
    store.start()
    field_out.wait()
    store.wait()


def local(
    u_now,
    u_prev,
    buoyancy,
    modulus,
    station_cell,
    path_class,
    spectra,
    cos_table,
    sin_table,
    path_filter,
    lf_basis,
    crossover,
):
    dma = pltpu.SemaphoreType.DMA
    anywhere = pl.BlockSpec(memory_space=pl.ANY)
    mine, other, samples, field = pl.pallas_call(
            kernel,
            out_shape=(
                jax.ShapeDtypeStruct((128, 512), F32),
                jax.ShapeDtypeStruct((128, 512), F32),
                jax.ShapeDtypeStruct((8, 128), F32),
                jax.ShapeDtypeStruct((128, 256), F32),
            ),
            in_specs=[anywhere] * 10,
            out_specs=(anywhere,) * 4,
            scratch_shapes=[
                pltpu.VMEM((1, 128), jnp.int32),
                pltpu.VMEM((128, 2048), jnp.int32),
                pltpu.VMEM((128, 512), BF16),
                pltpu.VMEM((128, 512), F32),
                pltpu.VMEM((128, 512), F32),
                pltpu.VMEM((8, 512), F32),
                pltpu.VMEM((128, 256), F32),
                pltpu.VMEM((8, 128), F32),
                pltpu.VMEM((16, 8, 128), jnp.int32),
                pltpu.VMEM((8, 128), jnp.int32),
                pltpu.VMEM((4, 8, 128), F32),
                pltpu.VMEM((2, 4, 8, 256), F32),
                pltpu.VMEM((2, 4, 8, 128), F32),
                pltpu.VMEM((4, 4, 8, 128), F32),
                pltpu.VMEM((4, 136, 384), F32),
                pltpu.VMEM((4, 256, 256), BF16),
                pltpu.VMEM((16, 8, 128), F32),
                pltpu.VMEM((16, 8, 128), F32),
                pltpu.VMEM((128, 2048), BF16),
                pltpu.VMEM((128, 2048), BF16),
                pltpu.VMEM((2, 912, 2048), BF16),
                pltpu.VMEM((2, 2, 64, 512), BF16),
                pltpu.VMEM((8, 2, 2, 64, 512), BF16),
                pltpu.VMEM((2, 128, 512), F32),
                dma((17,)),
                dma((16,)),
                dma((16,)),
                dma((8,)),
                dma((8,)),
                dma((16,)),
                dma((16,)),
                dma((12,)),
                dma((12,)),
                dma((12,)),
                dma((12,)),
                dma((28,)),
                dma((28,)),
                dma((4,)),
                dma((4,)),
            ],
            compiler_params=pltpu.CompilerParams(
                collective_id=0, has_side_effects=True, vmem_limit_bytes=60 * 1024 * 1024
            ),
        )(
            u_now,
            u_prev,
            buoyancy,
            modulus,
            station_cell.reshape(1, 128),
            path_class,
            spectra,
            cos_table,
            sin_table,
            path_filter,
    )
    return pl.pallas_call(
        merge,
        out_shape=(jax.ShapeDtypeStruct((128, 1024), F32), jax.ShapeDtypeStruct((128, 256), F32)),
        in_specs=[anywhere] * 6,
        out_specs=(anywhere,) * 2,
        scratch_shapes=[
            pltpu.VMEM((2, 128, 512), F32),
            pltpu.VMEM((8, 128), F32),
            pltpu.VMEM((4, 1024), F32),
            pltpu.VMEM((1, 512), F32),
            pltpu.VMEM((128, 1024), F32),
            pltpu.VMEM((128, 256), F32),
            dma((8,)),
        ],
        compiler_params=pltpu.CompilerParams(vmem_limit_bytes=60 * 1024 * 1024),
    )(mine, other, samples, field, lf_basis, crossover.reshape(1, 512))


def solution(mesh):
    in_specs = (
        P("grid", "sta"),
        P("grid", "sta"),
        P("grid", "sta"),
        P("grid", "sta"),
        P(("grid", "sta")),
        P(("grid", "sta"), None),
        P("sta", None),
        P("sta", None),
        P("sta", None),
        P(),
        P(),
        P(),
    )
    out_specs = (P(("grid", "sta"), None), P("grid", "sta"))
    return jax.shard_map(local, mesh=mesh, in_specs=in_specs, out_specs=out_specs, check_vma=False)
```

```python
import functools

import jax
import jax.numpy as jnp
from jax import lax
from jax.experimental import pallas as pl
from jax.experimental.pallas import tpu as pltpu
from jax.sharding import PartitionSpec as P

STEPS = 4
CLASSES = 8
MESH = pl.DeviceIdType.MESH
BF16 = jnp.bfloat16
F32 = jnp.float32

SLOTS = ((0, 0), (0, 1), (1, 0), (3, 0), (1, 1), (3, 1), (2, 0), (2, 1))
SIDES = [(0, -1), (0, 1), (-1, -1), (-1, 1), (1, -1), (1, 1)]
HALO = [(-1, 0), (1, 0)] + SIDES
FORWARDED = ((6, 0, 0), (6, 0, 1), (5, 0, 0), (4, 0, 1))
TILT = (0, 0, 2, 1, 0, 2, 0, 0)
GRID = 16
FARTHEST = (8, 9, 7, 10, 6, 11, 5, 12, 4, 13, 3, 14, 2, 15, 1, 0)
SUBCHIP = 256


def kernel(
    u_ref,
    up_ref,
    b_ref,
    m_ref,
    cell_ref,
    class_ref,
    spectra_ref,
    cos_ref,
    sin_ref,
    filter_ref,
    mine_ref,
    other_ref,
    samples_ref,
    field_ref,
    cellraw,
    classraw,
    spectra,
    cosines,
    sines,
    filters,
    final,
    total_samples,
    cells,
    cellsrc,
    colsrc,
    rowin,
    colin,
    cornerin,
    ext,
    ush,
    sampsrc,
    sampin,
    classown,
    classsib,
    onehot,
    phased,
    pieces,
    high,
    load_sem,
    cell_send,
    cell_recv,
    halo_send,
    halo_recv,
    samp_send,
    samp_recv,
    near_send,
    near_recv,
    relay_send,
    relay_recv,
    plane_send,
    plane_recv,
    sib_send,
    sib_recv,
):
    g = lax.axis_index("grid")
    s = lax.axis_index("sta")
    z, xl = g // 2, g % 2
    y, xh, core = s // 4, (s // 2) % 2, s % 2
    colour = (z + xl) % 2

    def along_grid(r):
        return ((g + r) % GRID, s)

    def beside(dg, ds):
        return ((g + dg + 16) % 16, (s + ds + 16) % 16)

    def chip(dy, cross, dc):
        xh2 = (xh + cross) % 2
        xl2 = (xl + cross) % 2
        return (z * 2 + xl2, (((y + dy) % 4) * 2 + xh2) * 2 + (core + dc) % 2)

    sibling = chip(0, 0, 1)
    plane = [((g + 2) % 16, s), ((g + 14) % 16, s), (z * 2 + 1 - xl, s)]
    near = [(dy, cross, dc) for dy, cross in ((1, 0), (3, 0), (0, 1)) for dc in (0, 1)]
    partners = [chip(*o) for o in near] + [sibling]
    partners += [beside(*o) for o in SIDES]
    partners += [along_grid(r) for r in range(1, GRID)]
    barrier = pltpu.get_barrier_semaphore()
    for partner in partners:
        pl.semaphore_signal(barrier, inc=1, device_id=partner, device_id_type=MESH)

    def load(i, src, dst):
        copy = pltpu.make_async_copy(src, dst, load_sem.at[i])
        copy.start()
        return copy

    load_cell = load(0, cell_ref, cellraw)
    load_phase = [load(5, spectra_ref, spectra), load(6, cos_ref, cosines), load(7, sin_ref, sines)]
    load_grid = [
        load(1 + a, ref, ext.at[a, pl.ds(0, 128), pl.ds(0, 256)])
        for a, ref in enumerate((u_ref, up_ref, b_ref, m_ref))
    ]
    load_class = load(8, class_ref, classraw)
    load_filter = load(9, filter_ref, filters)

    load_cell.wait()
    cellsrc[...] = jnp.broadcast_to(cellraw[...], (8, 128))
    for copy in load_phase:
        copy.wait()
    wide = spectra[...].astype(F32)
    phased[0] = (wide * cosines[...]).astype(BF16).reshape(2, 64, 512)
    phased[1] = (wide * sines[...]).astype(BF16).reshape(2, 64, 512)
    lane = lax.broadcasted_iota(jnp.int32, (128, 128), 1)
    packed = jnp.zeros((128, 128), F32)
    for a in range(4):
        load_grid[a].wait()
        both = jnp.where(lane < 64, ext[a, 0:128, 0:128], ext[a, 0:128, 128:256])
        packed = jnp.where(lane // 8 == a, pltpu.roll(both, 8 * a + 4, 1), packed)
    colsrc[...] = jnp.transpose(packed)[0:32].reshape(4, 8, 128)

    def expand(which, classes):
        held = classes[...]
        for c in range(1, CLASSES):
            onehot[which, (c - 1) * 128 : c * 128, :] = jnp.where(held == BF16(c), BF16(1), BF16(0))
        onehot[which, 896:912, :] = jnp.ones((16, 2048), BF16)


    pl.semaphore_wait(barrier, len(partners))

    def remote(src, dst, send, recv, target):
        copy = pltpu.make_async_remote_copy(
            src_ref=src, dst_ref=dst, send_sem=send, recv_sem=recv, device_id=target, device_id_type=MESH
        )
        copy.start()
        return copy

    halo_copies = []
    for i, (dg, ds) in enumerate(HALO):
        side = 1 if dg == 1 else 0
        rows = pl.ds(120 * side, 8)
        if ds == 0:
            src, dst = ext.at[:, rows, pl.ds(0, 256)], rowin.at[side]
        elif dg == 0:
            src, dst = colsrc, colin.at[1 if ds == 1 else 0]
        else:
            half = 1 if ds == 1 else 0
            src, dst = ext.at[:, rows, pl.ds(half * 128, 128)], cornerin.at[side * 2 + half]
        halo_copies.append(remote(src, dst, halo_send.at[i], halo_recv.at[i], beside(dg, ds)))
    cell_copies = {
        GRID - r: remote(cellsrc, cells.at[GRID - r], cell_send.at[r], cell_recv.at[r], along_grid(r))
        for r in FARTHEST
        if r
    }
    near_copies = {}

    def send_near(turn):
        for i, (dy, cross, dc) in enumerate(near):
            slot = SLOTS.index(((4 - dy) % 4, cross))
            half = 1 - colour if cross else colour
            part = 1 - turn if dy == 3 else turn
            rows = pl.ds(32 * part, 32)
            near_copies[dy, cross, dc, part] = remote(
                phased.at[(core + dc) % 2, half, rows],
                pieces.at[slot, core, half, rows],
                near_send.at[2 * i + part],
                near_recv.at[2 * i + part],
                chip(dy, cross, dc),
            )

    send_near(0)
    sib_piece = remote(phased.at[1 - core], pieces.at[0, core], sib_send.at[0], sib_recv.at[0], sibling)

    relay_copies = {}

    def relay(source, dy, cross, slot, part):
        i = len(relay_copies)
        rows = pl.ds(32 * part, 32)
        relay_copies[slot, cross, part] = remote(
            pieces.at[source, :, colour, rows],
            pieces.at[slot, :, colour, rows],
            relay_send.at[i],
            relay_recv.at[i],
            chip(dy, cross, 0),
        )

    plane_copies = {}

    def share(slot, part, half):
        for quarter in (2 * part, 2 * part + 1):
            rows = pieces.at[slot, :, half, pl.ds(16 * quarter, 16)]
            i = (slot - 1) * 4 + quarter
            plane_copies[slot, quarter] = remote(rows, rows, plane_send.at[i], plane_recv.at[i], plane[(i + TILT[slot]) % 3])

    load_class.wait()
    for slot, (dy, cross) in enumerate(SLOTS):
        source = ((y + dy) % 4) * 2 + (xh + cross) % 2
        columns = pl.ds(pl.multiple_of(source * SUBCHIP, SUBCHIP), SUBCHIP)
        classown[:, slot * SUBCHIP : (slot + 1) * SUBCHIP] = classraw[:, columns].astype(F32).astype(BF16)
    sib_class = remote(classown, classsib, sib_send.at[1], sib_recv.at[1], sibling)
    expand(0, classown)
    pieces[0, core] = phased[core]
    cells[0] = cellsrc[...]

    sib_piece.wait_recv()
    send_near(1)
    sib_class.wait_recv()
    expand(1, classsib)
    load_filter.wait()

    results, stores = [], []

    def multiply(slot):
        for quarter in range(4):
            if (slot, quarter) in plane_copies:
                plane_copies[slot, quarter].wait_recv()
        for cross, part in ((0, 0), (0, 1), (1, 0), (1, 1)):
            if (slot, cross, part) in relay_copies and (slot, cross, part) not in FORWARDED:
                relay_copies[slot, cross, part].wait_recv()
        part = pl.ds(slot * SUBCHIP, SUBCHIP)
        for n in (0, 256):
            weights = pieces[slot, :, :, :, n : n + 256].reshape(SUBCHIP, 256)
            first = filters[0:1, n : n + 256]
            total = jnp.dot(onehot[0, 896:912, part], weights, preferred_element_type=F32)
            acc = first * total[0:1]
            for c in range(1, CLASSES):
                lhs = onehot[:, (c - 1) * 128 : c * 128, part].reshape(256, SUBCHIP)
                acc = acc + (filters[c : c + 1, n : n + 256] - first) * jnp.dot(
                    lhs, weights, preferred_element_type=F32
                )
            acc = acc.reshape(2, 128, 256)
            if slot == 0:
                high[:, :, n : n + 256] = acc
            else:
                high[:, :, n : n + 256] += acc
            if slot == 7:
                done = pl.ds(n, 256)
                i = 2 + n // 256
                results.append(
                    remote(high.at[1, :, done], other_ref.at[:, done], sib_send.at[i], sib_recv.at[i], sibling)
                )
                mine_out = pltpu.make_async_copy(high.at[0, :, done], mine_ref.at[:, done], load_sem.at[13 + i])
                mine_out.start()
                stores.append(mine_out)

    multiply(0)

    def arrived(dy, cross, part):
        for dc in (0, 1):
            near_copies[dy, cross, dc, part].wait_recv()

    arrived(1, 0, 0)
    relay(3, 1, 0, 6, 0)
    arrived(3, 0, 1)
    relay(2, 3, 0, 6, 1)
    arrived(0, 1, 0)
    share(3, 0, colour)
    share(2, 1, colour)
    share(1, 0, colour)

    for copy in halo_copies:
        copy.wait_recv()
    zero = F32(0)
    lane8 = lax.broadcasted_iota(jnp.int32, (8, 128), 1)
    sub8 = lax.broadcasted_iota(jnp.int32, (8, 128), 0)
    sub8w = lax.broadcasted_iota(jnp.int32, (8, 256), 0)
    below, above = g < 15, g > 0
    right, left = s < 15, s > 0
    sides = []
    for a in range(4):
        sides.append(
            jnp.where(sub8 < 4, jnp.where(left, colin[1, a], zero), jnp.where(right, colin[0, a], zero))
        )
    columns = jnp.transpose(jnp.concatenate(sides + [jnp.zeros((96, 128), F32)], axis=0))
    for a in range(4):
        ext[a, 0:128, 256:384] = pltpu.roll(columns, 128 - (8 * a + 4), 1)
        ext[a, 128:136, 0:256] = jnp.where(
            sub8w < 4, jnp.where(below, rowin[0, a], zero), jnp.where(above, rowin[1, a], zero)
        )
        ext[a, 128:136, 256:384] = jnp.where(
            sub8 < 4,
            jnp.where(
                lane8 < 64,
                jnp.where(below & right, cornerin[0, a], zero),
                jnp.where(below & left, cornerin[1, a], zero),
            ),
            jnp.where(
                lane8 < 64,
                jnp.where(above & right, cornerin[2, a], zero),
                jnp.where(above & left, cornerin[3, a], zero),
            ),
        )
    current, previous, buoyancy, modulus = ext[0], ext[1], ext[2], ext[3]
    rows, cols = current.shape
    down = 0.5 * (modulus + pltpu.roll(modulus, rows - 1, 0))
    along = 0.5 * (modulus + pltpu.roll(modulus, cols - 1, 1))
    for step in range(STEPS):
        flux_x = down * (pltpu.roll(current, rows - 1, 0) - current)
        flux_y = along * (pltpu.roll(current, cols - 1, 1) - current)
        div = flux_x - pltpu.roll(flux_x, 1, 0) + flux_y - pltpu.roll(flux_y, 1, 1)
        following = 2.0 * current - previous + buoyancy * div
        previous, current = current, following
        block = current[0:128, 0:256]
        coarse = block.astype(BF16)
        ush[step, 0:128, :] = coarse
        ush[step, 128:256, :] = (block - coarse.astype(F32)).astype(BF16)
        if step == STEPS - 1:
            final[...] = block

    field_out = pltpu.make_async_copy(final, field_ref, load_sem.at[13])
    field_out.start()

    for copy in ((1, 0, 1), (3, 0, 0), (0, 1, 1)):
        arrived(*copy)
    relay(1, 1, 0, 5, 0)
    relay(1, 3, 0, 4, 1)
    relay(3, 0, 1, 5, 1)
    relay(2, 0, 1, 4, 0)
    share(1, 1, colour)
    share(3, 1, colour)
    share(2, 0, colour)

    row_at = lax.broadcasted_iota(jnp.int32, (128, 128), 0)
    col_at = lax.broadcasted_iota(jnp.int32, (256, 128), 0)
    samp_copies = []

    def look_up(first, last):
        for pair in range(first, last, 2):
            pair = FARTHEST[pair : pair + 2]
            for r in pair:
                if r > 0:
                    cell_copies[r].wait_recv()
            picks, inside = [], []
            for r in pair:
                cell = cells[r, 0:1, :]
                row = lax.shift_right_logical(cell, 12) - g * 128
                col = lax.bitwise_and(cell, 4095) - s * 256
                picks.append(jnp.where(col_at == col, F32(1), zero).astype(BF16))
                inside.append(row_at == row)
            found = jnp.dot(
                ush[...].reshape(4 * 256, 256), jnp.concatenate(picks, axis=1), preferred_element_type=F32
            )
            mask = jnp.concatenate(inside, axis=1)
            recorded = []
            for step in range(STEPS):
                both = found[step * 256 : step * 256 + 128] + found[step * 256 + 128 : step * 256 + 256]
                recorded.append(jnp.sum(jnp.where(mask, both, zero), axis=0, keepdims=True))
            recorded = jnp.concatenate(recorded + [jnp.zeros((4, 256), F32)], axis=0)
            sampsrc[pair[0]] = recorded[:, 0:128]
            sampsrc[pair[1]] = recorded[:, 128:256]
            for r in pair:
                if r > 0:
                    samp_copies.append(
                        remote(sampsrc.at[r], sampin.at[GRID - r], samp_send.at[r], samp_recv.at[r], along_grid(r))
                    )

    look_up(0, GRID // 2)

    relay(1, 1, 0, 5, 1)
    relay(1, 3, 0, 4, 0)
    relay_copies[6, 0, 0].wait_recv()
    relay(6, 0, 1, 7, 0)
    relay_copies[6, 0, 1].wait_recv()
    relay(6, 0, 1, 7, 1)
    share(6, 0, colour)
    share(6, 1, colour)
    look_up(GRID // 2, GRID)
    relay_copies[5, 0, 0].wait_recv()
    relay(5, 1, 0, 7, 0)
    relay_copies[4, 0, 1].wait_recv()
    relay(4, 3, 0, 7, 1)
    share(5, 0, colour)
    share(4, 1, colour)
    for slot in (1, 2, 3, 6, 5, 4, 7):
        multiply(slot)

    for copy in samp_copies:
        copy.wait_recv()
    samples = sampsrc[0]
    for r in range(1, GRID):
        samples = samples + sampin[r]
    total_samples[...] = samples
    samples_out = pltpu.make_async_copy(total_samples, samples_ref, load_sem.at[14])
    samples_out.start()
    for copy in results:
        copy.wait_recv()
    for copy in stores:
        copy.wait()
    samples_out.wait()
    field_out.wait()

    sent = halo_copies + list(cell_copies.values()) + samp_copies + list(near_copies.values()) + list(relay_copies.values())
    sent += list(plane_copies.values())
    for copy in sent + [sib_piece, sib_class] + results:
        copy.wait_send()


def merge(
    mine_ref,
    other_ref,
    samples_ref,
    field_ref,
    basis_ref,
    cross_ref,
    out_ref,
    ufinal_ref,
    halves,
    samples,
    bases,
    crossing,
    out,
    field,
    sem,
):
    core = lax.axis_index("sta") % 2
    field_in = pltpu.make_async_copy(field_ref, field, sem.at[0])
    field_out = pltpu.make_async_copy(field, ufinal_ref, sem.at[7])
    loads = [
        pltpu.make_async_copy(samples_ref, samples, sem.at[1]),
        pltpu.make_async_copy(basis_ref, bases, sem.at[2]),
        pltpu.make_async_copy(cross_ref, crossing, sem.at[3]),
    ]
    halves_in = [
        pltpu.make_async_copy(mine_ref, halves.at[core], sem.at[4]),
        pltpu.make_async_copy(other_ref, halves.at[1 - core], sem.at[5]),
    ]
    for copy in loads:
        copy.start()
    for copy in halves_in:
        copy.start()
    field_in.start()
    for copy in loads:
        copy.wait()
    across = jnp.transpose(jnp.concatenate([samples[...], jnp.zeros((120, 128), F32)], axis=0))
    basis = bases[...]
    lowpass = jnp.concatenate([crossing[...], crossing[...]], axis=1)
    weight = lowpass * (1.0 - lowpass)
    low = across[:, 0:1] * basis[0:1, :]
    for step in range(1, STEPS):
        low = low + across[:, step : step + 1] * basis[step : step + 1, :]
    numer = jnp.sum(weight * low * low, axis=1, keepdims=True) * (1.0 / 1024)
    field_in.wait()
    field_out.start()
    for copy in halves_in:
        copy.wait()
    full = jnp.concatenate([halves[0], halves[1]], axis=1)
    denom = jnp.sum(weight * full * full, axis=1, keepdims=True) * (1.0 / 1024)
    ratio = jnp.sqrt((numer + 1e-06) / (denom + 1e-06))
    out[...] = lowpass * low + (1.0 - lowpass) * (ratio * full)
    store = pltpu.make_async_copy(out, out_ref, sem.at[6])
    store.start()
    field_out.wait()
    store.wait()


def local(
    u_now,
    u_prev,
    buoyancy,
    modulus,
    station_cell,
    path_class,
    spectra,
    cos_table,
    sin_table,
    path_filter,
    lf_basis,
    crossover,
):
    dma = pltpu.SemaphoreType.DMA
    anywhere = pl.BlockSpec(memory_space=pl.ANY)
    mine, other, samples, field = pl.pallas_call(
            kernel,
            out_shape=(
                jax.ShapeDtypeStruct((128, 512), F32),
                jax.ShapeDtypeStruct((128, 512), F32),
                jax.ShapeDtypeStruct((8, 128), F32),
                jax.ShapeDtypeStruct((128, 256), F32),
            ),
            in_specs=[anywhere] * 10,
            out_specs=(anywhere,) * 4,
            scratch_shapes=[
                pltpu.VMEM((1, 128), jnp.int32),
                pltpu.VMEM((128, 2048), jnp.int32),
                pltpu.VMEM((128, 512), BF16),
                pltpu.VMEM((128, 512), F32),
                pltpu.VMEM((128, 512), F32),
                pltpu.VMEM((8, 512), F32),
                pltpu.VMEM((128, 256), F32),
                pltpu.VMEM((8, 128), F32),
                pltpu.VMEM((16, 8, 128), jnp.int32),
                pltpu.VMEM((8, 128), jnp.int32),
                pltpu.VMEM((4, 8, 128), F32),
                pltpu.VMEM((2, 4, 8, 256), F32),
                pltpu.VMEM((2, 4, 8, 128), F32),
                pltpu.VMEM((4, 4, 8, 128), F32),
                pltpu.VMEM((4, 136, 384), F32),
                pltpu.VMEM((4, 256, 256), BF16),
                pltpu.VMEM((16, 8, 128), F32),
                pltpu.VMEM((16, 8, 128), F32),
                pltpu.VMEM((128, 2048), BF16),
                pltpu.VMEM((128, 2048), BF16),
                pltpu.VMEM((2, 912, 2048), BF16),
                pltpu.VMEM((2, 2, 64, 512), BF16),
                pltpu.VMEM((8, 2, 2, 64, 512), BF16),
                pltpu.VMEM((2, 128, 512), F32),
                dma((17,)),
                dma((16,)),
                dma((16,)),
                dma((8,)),
                dma((8,)),
                dma((16,)),
                dma((16,)),
                dma((12,)),
                dma((12,)),
                dma((12,)),
                dma((12,)),
                dma((28,)),
                dma((28,)),
                dma((4,)),
                dma((4,)),
            ],
            compiler_params=pltpu.CompilerParams(
                collective_id=0, has_side_effects=True, vmem_limit_bytes=60 * 1024 * 1024
            ),
        )(
            u_now,
            u_prev,
            buoyancy,
            modulus,
            station_cell.reshape(1, 128),
            path_class,
            spectra,
            cos_table,
            sin_table,
            path_filter,
    )
    return pl.pallas_call(
        merge,
        out_shape=(jax.ShapeDtypeStruct((128, 1024), F32), jax.ShapeDtypeStruct((128, 256), F32)),
        in_specs=[anywhere] * 6,
        out_specs=(anywhere,) * 2,
        scratch_shapes=[
            pltpu.VMEM((2, 128, 512), F32),
            pltpu.VMEM((8, 128), F32),
            pltpu.VMEM((4, 1024), F32),
            pltpu.VMEM((1, 512), F32),
            pltpu.VMEM((128, 1024), F32),
            pltpu.VMEM((128, 256), F32),
            dma((8,)),
        ],
        compiler_params=pltpu.CompilerParams(vmem_limit_bytes=60 * 1024 * 1024),
    )(mine, other, samples, field, lf_basis, crossover.reshape(1, 512))


def solution(mesh):
    in_specs = (
        P("grid", "sta"),
        P("grid", "sta"),
        P("grid", "sta"),
        P("grid", "sta"),
        P(("grid", "sta")),
        P(("grid", "sta"), None),
        P("sta", None),
        P("sta", None),
        P("sta", None),
        P(),
        P(),
        P(),
    )
    out_specs = (P(("grid", "sta"), None), P("grid", "sta"))
    return jax.shard_map(local, mesh=mesh, in_specs=in_specs, out_specs=out_specs, check_vma=False)
```
